512 devices in a mesh: dp: 8 (over y_hi, core), sp: 64 (over z, y_lo, x).
Axes of the slice: x: 4, y: 8 (y_hi: 4, y_lo: 2; y = y_hi * 2 + y_lo), z: 8, core: 2. Of those that a mesh axis runs over, the one named last changes fastest.
Arguments:
- query: bfloat16 [8, 256, 64, 576], P('dp', 'sp'), may hold values from -320 to 320
- latent: bfloat16 [8, 4096, 576], P('dp', 'sp'), may hold values from -6 to 6
- dout: bfloat16 [8, 256, 64, 512], P('dp', 'sp'), may hold values from -6 to 6
- hidden: bfloat16 [8, 4096, 7168], P('dp', 'sp'), may hold values from -0.119628906 to 0.119628906
Outputs:
- dquery: bfloat16 [8, 256, 64, 576], P('dp', 'sp')
- dlatent: float32 [8, 4096, 576], P('dp', 'sp')
- dweight: float32 [7168, 64], P(('dp', 'sp'))
The draws below stay inside these ranges and needn't reach their ends.
All inputs are finite; a program needn't handle non-finite values.
Results may differ from the reference program's by a relative error of at most 0.039.
Values may be sent and summed in bfloat16 or wider, within the bound.
No kernel may reach another device: no remote copies, remote signals or barrier semaphores. Data moves between devices by JAX's collectives and lax.ppermute only.
A program may use at most 128 MiB of HBM per device.

```python
import jax
import jax.numpy as jnp
from jax import lax

H = 64
LAT = 512
ROPE = 64
D = 7168
QTOT = 256
KTOT = 4096
SEQS = 8


def shared_rope(key):
    return jnp.clip(jax.random.normal(key, (SEQS, KTOT, ROPE), jnp.float32), -4.0, 4.0)


def draw_latent(key, part):
    rope = shared_rope(key)
    key = jax.random.fold_in(key, 3)
    first = jax.random.fold_in(key, 0)
    front = jnp.clip(jax.random.normal(first, (SEQS, KTOT, LAT), jnp.float32), -6.0, 6.0)
    return jnp.concatenate([front, rope], axis=2).astype(jnp.bfloat16)


def draw_query(key, part):
    key = jax.random.fold_in(key, 11)
    first = jax.random.fold_in(key, 0)
    base = 0.6 * jnp.clip(jax.random.normal(first, (SEQS, QTOT, H, LAT + ROPE), jnp.float32), -6.0, 6.0)
    return base.astype(jnp.bfloat16)


def block_scale(key, shape, cuts, least, top_value):
    def one(dim, parts):
        steps = jax.random.uniform(jax.random.fold_in(jax.random.fold_in(key, 6), dim), (parts,), jnp.float32, least / len(cuts), top_value / len(cuts))
        return jnp.repeat(jnp.exp(steps), shape[dim] // parts).reshape((-1,) + (1,) * (len(shape) - dim - 1))

    factor_of = one(*cuts[0])
    for cut in cuts[1:]:
        factor_of = factor_of * one(*cut)
    return factor_of


def normal_values(rng, dims, spread, reach, pieces=(), held_as=jnp.bfloat16):
    entries = jax.random.normal(rng, dims, jnp.float32) * spread
    if len(pieces) > 0:
        entries = block_scale(rng, dims, pieces, -0.22, 0.18) * entries
    return jnp.clip(entries, min=-reach, max=reach).astype(held_as)


def setup_inputs(seed: int = 0) -> dict:
    keys = jax.random.split(jax.random.key(seed), 5)
    return {
        "query": draw_query(jax.random.fold_in(keys[4], 71), 0),
        "latent": draw_latent(jax.random.fold_in(keys[4], 71), 0),
        "dout": normal_values(keys[2], (SEQS, QTOT, H, LAT), 1.0, 6.0, ((0, 8), (1, 64))),
        "hidden": normal_values(keys[3], (SEQS, KTOT, D), 0.02, 0.119628906, ((0, 8), (1, 64))),
    }


softmax_scale = 0.07216878364870323

def head_grad(query_head, dout_head, latent_seq, allowed):
    scores = jnp.dot(query_head, latent_seq.T, preferred_element_type=jnp.float32) * softmax_scale
    scores = jnp.where(allowed, scores, -jnp.inf)
    top = lax.optimization_barrier(jnp.max(scores, axis=1, keepdims=True))
    expd = jnp.exp(scores - top)
    probs = expd / lax.optimization_barrier(jnp.sum(expd, axis=1, keepdims=True))
    probs_low = probs.astype(jnp.bfloat16)
    value = latent_seq[:, :LAT]
    out = jnp.dot(probs_low, value, preferred_element_type=jnp.float32)
    delta = lax.optimization_barrier(jnp.sum(dout_head.astype(jnp.float32) * out, axis=1, keepdims=True))
    dprobs = jnp.dot(dout_head, value.T, preferred_element_type=jnp.float32)
    dscores_low = (probs * (dprobs - delta)).astype(jnp.bfloat16)
    dq = (jnp.dot(dscores_low, latent_seq, preferred_element_type=jnp.float32) * softmax_scale).astype(jnp.bfloat16)
    from_scores = jnp.dot(dscores_low.T, query_head, preferred_element_type=jnp.float32) * softmax_scale
    from_values = jnp.dot(probs_low.T, dout_head, preferred_element_type=jnp.float32)
    dlat = from_scores + jnp.pad(from_values, ((0, 0), (0, ROPE)))
    return (dq, dlat)

def reference(query, latent, dout, hidden):
    qpos = jnp.arange(QTOT, dtype=jnp.int32) + (KTOT - QTOT)
    kpos = jnp.arange(KTOT, dtype=jnp.int32)
    allowed = kpos[None, :] <= qpos[:, None]

    def one_seq(items):
        query_seq, dout_seq, latent_seq = items

        def step(carry, head_items):
            dq, dlat = head_grad(head_items[0], head_items[1], latent_seq, allowed)
            return (carry + dlat, dq)
        init = jnp.zeros((KTOT, LAT + ROPE), jnp.float32)
        total, dq_heads = lax.scan(step, init, (jnp.swapaxes(query_seq, 0, 1), jnp.swapaxes(dout_seq, 0, 1)))
        return (jnp.swapaxes(dq_heads, 0, 1), total)
    dquery, dlatent = lax.map(one_seq, (query, dout, latent))
    rope_low = dlatent[:, :, LAT:].astype(jnp.bfloat16)
    dweight = jnp.dot(hidden.reshape(SEQS * KTOT, D).T, rope_low.reshape(SEQS * KTOT, ROPE), preferred_element_type=jnp.float32)
    return (dquery, dlatent, dweight)
```

```python
import jax
import jax.numpy as jnp
from jax import lax
from jax.sharding import Mesh, PartitionSpec as P

softmax_scale = 0.07216878364870323
f32, bf16 = jnp.float32, jnp.bfloat16


def fetch(value, offset, n):
    return lax.ppermute(value, "x", [(s, (s - offset) % n) for s in range(n)])


def spread(value, axes, n):
    return lax.all_to_all(
        jnp.broadcast_to(value[None], (n,) + value.shape), axes, 0, 0, tiled=True
    )


def body(query, latent, dout, hidden):
    nd, nz, ny, nx = (lax.axis_size(a) for a in ("dp", "z", "y", "x"))
    grp = nz * ny
    tok, heads, width = query.shape[1:]
    lat_width = dout.shape[3]
    rope_width = width - lat_width
    k_dev, model = hidden.shape[1:]
    rows = tok * heads
    k_total = k_dev * grp * nx
    q_total = tok * grp * nx
    z, y, x = (lax.axis_index(a) for a in ("z", "y", "x"))
    q0 = query.reshape(rows, width)
    o0 = dout.reshape(rows, lat_width)
    keys = spread(latent[0], ("z", "y"), grp).reshape(grp * k_dev, width)
    q = jnp.concatenate([q0] + [fetch(q0, k, nx) for k in range(1, nx)])
    o = jnp.concatenate([o0] + [fetch(o0, k, nx) for k in range(1, nx)])
    value = keys[:, :lat_width]
    block = model // (nd * grp * nx)
    cols = hidden[0].reshape(k_dev, nd, grp, nx * block).transpose(2, 0, 1, 3)
    cols = cols.reshape(grp, k_dev, nd * nx * block)
    cols = lax.all_to_all(cols, ("z", "y"), 0, 0, tiled=True).reshape(grp * k_dev, -1)

    n_rows, n_keys = nx * rows, grp * k_dev
    r = jnp.arange(n_rows, dtype=jnp.int32)
    owner = lax.rem(x + r // rows, nx)
    q_pos = ((z * ny + y) * nx + owner) * tok + (r % rows) // heads
    j = jnp.arange(n_keys, dtype=jnp.int32)
    k_pos = ((j // k_dev) * nx + x) * k_dev + j % k_dev
    s = lax.dot_general(q, keys, (((1,), (1,)), ((), ())), preferred_element_type=f32)
    s = s * softmax_scale
    s = jnp.where(k_pos[None, :] <= q_pos[:, None] + (k_total - q_total), s, -jnp.inf)
    m = jnp.max(s, axis=1)
    e = jnp.exp(s - m[:, None])
    l = jnp.sum(e, axis=1)
    dp = lax.dot_general(o, value, (((1,), (1,)), ((), ())), preferred_element_type=f32)
    d = jnp.sum(e * dp, axis=1)
    mine = jnp.stack([m, l, d]).reshape(3, nx, rows)
    stats = [mine]
    for k in range(1, nx):
        stats.append(jnp.roll(fetch(mine, k, nx), k, axis=1))
    stats = jnp.stack(stats).reshape(nx, 3, n_rows)
    top = jnp.max(stats[:, 0], axis=0)
    w = jnp.exp(stats[:, 0] - top)
    total = jnp.sum(stats[:, 1] * w, axis=0)
    delta = jnp.sum(stats[:, 2] * w, axis=0) / total
    f = jnp.exp(m - top) / total
    p = e * f[:, None]
    p_low = p.astype(bf16)
    ds = (p * (dp - delta[:, None])).astype(bf16)

    def down(a, b):
        return lax.dot_general(a, b, (((0,), (0,)), ((), ())), preferred_element_type=f32)

    rope = (down(ds, q[:, lat_width:]) * softmax_scale).astype(bf16)
    rope = lax.all_to_all(rope.reshape(grp, k_dev, rope_width), ("z", "y"), 0, 0, tiled=True)
    rope = jnp.sum(rope.astype(f32), axis=0)
    rope_all = spread(rope.astype(bf16), ("z", "y"), grp).reshape(n_keys, rope_width)
    terms = down(cols, rope_all).reshape(nd, nx, block, rope_width)
    terms = lax.all_to_all(terms.reshape(nd * nx, block, rope_width), ("dp", "x"), 0, 0, tiled=True)
    dweight = jnp.sum(terms, axis=0)

    lat = (down(ds, q[:, :lat_width]) * softmax_scale + down(p_low, o)).astype(bf16)
    lat = lax.all_to_all(lat.reshape(grp, k_dev, lat_width), ("z", "y"), 0, 0, tiled=True)
    lat = jnp.sum(lat.astype(f32), axis=0)
    dlatent = jnp.concatenate([lat, rope], axis=1)[None]

    dq = jnp.dot(ds, keys, preferred_element_type=f32) * softmax_scale
    total_q = dq[:rows]
    parts = [fetch(dq[k * rows : (k + 1) * rows].astype(bf16), nx - k, nx) for k in range(1, nx)]
    for part in parts:
        total_q = total_q + part.astype(f32)
    dquery = total_q.astype(bf16).reshape(1, tok, heads, width)
    return dquery, dlatent, dweight


def solution(mesh):
    fine = Mesh(mesh.devices.reshape(8, 8, 2, 4), ("dp", "z", "y", "x"))
    sp = ("z", "y", "x")
    in_specs = (
        P("dp", sp, None, None),
        P("dp", sp, None),
        P("dp", sp, None, None),
        P("dp", sp, None),
    )
    out_specs = (P("dp", sp, None, None), P("dp", sp, None), P(("dp",) + sp, None))
    return jax.shard_map(body, mesh=fine, in_specs=in_specs, out_specs=out_specs, check_vma=False)
```

```python
import functools

import jax
import jax.numpy as jnp
from jax import lax
from jax.experimental import pallas as pl
from jax.experimental.pallas import tpu as pltpu
from jax.sharding import Mesh, PartitionSpec as P

softmax_scale = 0.07216878364870323
f32, bf16 = jnp.float32, jnp.bfloat16
TILE = 256
SLOT = 16


def nt(a, b):
    return lax.dot_general(a, b, (((1,), (1,)), ((), ())), preferred_element_type=f32)


def nn(a, b):
    return lax.dot_general(a, b, (((1,), (0,)), ((), ())), preferred_element_type=f32)


def tn(a, b):
    return lax.dot_general(a, b, (((0,), (0,)), ((), ())), preferred_element_type=f32)


def call(kernel, outs, n_in, smem=(), unused=(), flops=0, moved=0, limit=48):
    vmem = pl.BlockSpec(memory_space=pltpu.VMEM)
    specs = [
        pl.BlockSpec(memory_space=pltpu.SMEM)
        if i in smem
        else (pl.BlockSpec(memory_space=pl.ANY) if i in unused else vmem)
        for i in range(n_in)
    ]
    return pl.pallas_call(
        kernel,
        out_shape=[jax.ShapeDtypeStruct(s, d) for s, d in outs],
        in_specs=specs,
        out_specs=[vmem] * len(outs),
        compiler_params=pltpu.CompilerParams(vmem_limit_bytes=limit * 2**20),
        cost_estimate=pl.CostEstimate(flops=flops, bytes_accessed=moved, transcendentals=0),
    )


def pack_kernel(dout, query, out):
    lat = dout.shape[1]
    width = query.shape[1]
    out[:, :lat] = dout[...]
    out[:, lat : lat + width] = query[...]
    out[:, lat + width :] = jnp.zeros((out.shape[0], out.shape[1] - lat - width), out.dtype)


def row_blocks(refs):
    own, right, first, second, left = refs
    return [
        lambda c: own[:, c],
        lambda c: right[:, c],
        lambda c: jnp.concatenate([first[:, c], second[:, c]]),
        lambda c: left[:, c],
    ]


def columns_kernel(block, n_z, n_grp, hid, after, after2, after3, out):
    k_dev, model = hid.shape
    n_data = model // (n_z * n_grp * block)
    span = n_z * n_grp * block
    wide = n_z * SLOT
    c = lax.broadcasted_iota(jnp.int32, (span, n_grp * wide), 0)
    o = lax.broadcasted_iota(jnp.int32, (span, n_grp * wide), 1)
    g, zz, k = o // wide, (o % wide) // SLOT, o % SLOT
    pick = jnp.where((c == (zz * n_grp + g) * block + k) & (k < block), 1.0, 0.0).astype(bf16)
    stacked = jnp.concatenate([hid[:, d * span : (d + 1) * span] for d in range(n_data)])
    moved = nn(stacked, pick).astype(bf16)
    for d in range(n_data):
        for g in range(n_grp):
            out[g, :, d * wide : (d + 1) * wide] = moved[
                d * k_dev : (d + 1) * k_dev, g * wide : (g + 1) * wide
            ]


def key_tile(near, far, i, per):
    ref, first = (near, i * per) if i * per < near.shape[0] else (far, i * per - near.shape[0])
    k = ref[first : first + per]
    return k.reshape(k.shape[0] * k.shape[1], k.shape[2])


def scores_kernel(lat, heads, pos, near, far, *refs):
    blocks, (e_ref, dp_ref, st_ref) = row_blocks(refs[1:-3]), refs[-3:]
    z, y, x = pos[0], pos[1], pos[2]
    n_z, k_dev, _ = near.shape
    n_x = len(blocks)
    rows = refs[1].shape[0]
    n_keys = 2 * n_z * k_dev
    tiles = n_keys // TILE
    per = TILE // k_dev
    tok = rows // heads
    first_query = n_z * 2 * n_x * (k_dev - tok)
    for b, t in enumerate(blocks):
        q, o = t(slice(lat, lat + near.shape[2])), t(slice(0, lat))
        cols = slice(b * rows, (b + 1) * rows)
        lane = lax.broadcasted_iota(jnp.int32, (k_dev, rows), 1)
        q_pos = ((z * 2 + y) * n_x + lax.rem(x + b, n_x)) * tok + lane // heads + first_query
        top = None
        for i in range(tiles):
            s = nt(key_tile(near, far, i, per), q) * softmax_scale
            half, zz = divmod((i + 1) * per - 1, n_z)
            if zz == n_z - 1:
                side = y if half == 0 else 1 - y
                k_pos = ((zz * 2 + side) * n_x + x) * k_dev + lax.broadcasted_iota(
                    jnp.int32, (k_dev, rows), 0
                )
                last = jnp.where(k_pos <= q_pos, s[TILE - k_dev :], -jnp.inf)
                s = jnp.concatenate([s[: TILE - k_dev], last])
            e_ref[i * TILE : (i + 1) * TILE, cols] = s
            m = jnp.max(s, axis=0, keepdims=True)
            top = m if top is None else jnp.maximum(top, m)
        total = jnp.zeros_like(top)
        delta = jnp.zeros_like(top)
        for i in range(tiles):
            part = slice(i * TILE, (i + 1) * TILE)
            dp = nt(key_tile(near, far, i, per)[:, :lat], o)
            e = jnp.exp(e_ref[part, cols] - top)
            e_ref[part, cols] = e
            dp_ref[part, cols] = dp
            total += jnp.sum(e, axis=0, keepdims=True)
            delta += jnp.sum(e * dp, axis=0, keepdims=True)
        st_ref[4 * b : 4 * b + 4] = jnp.concatenate([top, total, delta, jnp.zeros_like(top)])


def copies_kernel(st, after, out):
    out[...] = jnp.broadcast_to(st[...][None], out.shape)


def dscores_kernel(lat, pos, stats, st, e_ref, dp_ref, *refs):
    blocks, (p_ref, ds_ref, rope_ref) = row_blocks(refs[:-3]), refs[-3:]
    y, x = pos[1], pos[2]
    n_x = len(blocks)
    rows = refs[0].shape[0]
    tiles = e_ref.shape[0] // TILE
    grp, half_keys, _ = rope_ref.shape
    k_dev = 2 * half_keys
    for b in range(n_x):
        cols = slice(b * rows, (b + 1) * rows)
        theirs = []
        for s in range(n_x):
            at = lax.rem(x + b + n_x - s, n_x)
            v = stats[s, 0:4]
            for j in range(1, n_x):
                v = jnp.where(at == j, stats[s, 4 * j : 4 * j + 4], v)
            theirs.append(v)
        top = functools.reduce(jnp.maximum, [v[0:1] for v in theirs])
        w = [jnp.exp(v[0:1] - top) for v in theirs]
        total = sum(v[1:2] * u for v, u in zip(theirs, w))
        delta = sum(v[2:3] * u for v, u in zip(theirs, w)) / total
        f = jnp.exp(st[4 * b : 4 * b + 1] - top) / total
        for i in range(tiles):
            part = slice(i * TILE, (i + 1) * TILE)
            p = e_ref[part, cols] * f
            p_ref[part, cols] = p.astype(bf16)
            ds_ref[part, cols] = (p * (dp_ref[part, cols] - delta)).astype(bf16)
    n_z = grp // 2
    for i in range(tiles):
        part = slice(i * TILE, (i + 1) * TILE)
        r = None
        for b, t in enumerate(blocks):
            q = t(slice(2 * lat, 2 * lat + rope_ref.shape[2] // 2))
            v = nn(ds_ref[part, b * rows : (b + 1) * rows], q)
            r = v if r is None else r + v
        r = (r * softmax_scale).astype(bf16)
        for j in range(TILE // k_dev):
            half, zz = divmod(i * (TILE // k_dev) + j, n_z)
            side = y if half == 0 else 1 - y
            k = r[j * k_dev : (j + 1) * k_dev]
            rope_ref[2 * zz + side] = jnp.concatenate([k[:half_keys], k[half_keys:]], axis=1)


def grads_kernel(lat, p_ref, ds_ref, near, far, *refs):
    blocks, (mine, other), dq_refs = row_blocks(refs[:5]), refs[5:7], refs[7:]
    n_z, k_dev, _ = near.shape
    rows = refs[0].shape[0]
    tiles = p_ref.shape[0] // TILE
    per = TILE // k_dev
    for i in range(tiles):
        part = slice(i * TILE, (i + 1) * TILE)
        v = None
        for b, t in enumerate(blocks):
            a = nn(ds_ref[part, b * rows : (b + 1) * rows], t(slice(lat, 2 * lat)))
            v = a if v is None else v + a
        v = v * softmax_scale
        for b, t in enumerate(blocks):
            v += nn(p_ref[part, b * rows : (b + 1) * rows], t(slice(0, lat)))
        out, first = (mine, i * per) if i * per < n_z else (other, i * per - n_z)
        out[first : first + per] = v.astype(bf16).reshape(per, k_dev, lat)
    for b, out in enumerate(dq_refs):
        v = None
        for i in range(tiles):
            a = tn(
                ds_ref[i * TILE : (i + 1) * TILE, b * rows : (b + 1) * rows],
                key_tile(near, far, i, per),
            )
            v = a if v is None else v + a
        out[...] = (v * softmax_scale).astype(out.dtype)


def rope_kernel(parts, all_ref, rope_ref):
    half = parts.shape[1]
    v = jnp.sum(parts[...].astype(f32), axis=0)
    rope_ref[...] = jnp.concatenate([v[:, : v.shape[1] // 2], v[:, v.shape[1] // 2 :]])
    all_ref[...] = jnp.broadcast_to(v.astype(bf16)[None], all_ref.shape)


def weight_kernel(cols, rope, out):
    n, k_dev, wide = cols.shape
    e = rope.shape[2] // 2
    r = jnp.concatenate([rope[:, :, :e], rope[:, :, e:]], axis=1).reshape(n * k_dev, e)
    v = tn(cols[...].reshape(n * k_dev, wide), r).reshape(wide // SLOT, SLOT, e)
    out[...] = jnp.concatenate([v[:, : SLOT // 2], v[:, SLOT // 2 :]], axis=2)


def weight_sum_kernel(parts, out):
    v = jnp.sum(parts[...], axis=0)
    e = v.shape[1] // 2
    out[...] = jnp.concatenate([v[:, :e], v[:, e:]])[: out.shape[0]]


def latent_sum_kernel(parts, rope, out):
    lat = parts.shape[2]
    out[:, :lat] = jnp.sum(parts[...].astype(f32), axis=0)
    out[:, lat:] = rope[...]


def fetch(value, offset, n):
    return lax.ppermute(value, "x", [(s, (s - offset) % n) for s in range(n)])


def trade(value, axes):
    return lax.all_to_all(value, axes, 0, 0, tiled=True)


def body(query, latent, dout, hidden):
    nd, nz, ny, nx = (lax.axis_size(a) for a in ("dp", "z", "y", "x"))
    tok, heads, width = query.shape[1:]
    lat = dout.shape[3]
    rope = width - lat
    k_dev, model = hidden.shape[1:]
    rows = tok * heads
    n_rows, n_keys = nx * rows, nz * ny * k_dev
    block = model // (nd * nz * ny * nx)
    pos = jnp.stack([lax.axis_index(a) for a in ("z", "y", "x")]).astype(jnp.int32)

    near = trade(jnp.broadcast_to(latent, (nz, k_dev, width)), "z")
    (own,) = call(pack_kernel, [((rows, -(-(lat + width) // 128) * 128), bf16)], 2, moved=4 * rows * width)(
        dout.reshape(rows, lat), query.reshape(rows, width)
    )
    right, left = fetch(own, 1, nx), fetch(own, nx - 1, nx)
    first, second = fetch(right[: rows // 2], 1, nx), fetch(left[rows // 2 :], nx - 1, nx)
    blocks = [own, right, first, second, left]
    far = lax.ppermute(near, "y", [(0, 1), (1, 0)])

    wide = nd * nz * SLOT
    (cols,) = call(
        functools.partial(columns_kernel, block, nz, ny * nx),
        [((ny * nx, k_dev, wide), bf16)], 4, unused=(1, 2, 3),
        flops=2 * k_dev * nd * (model // nd) * 1024, moved=2 * k_dev * model * 2,
    )(hidden[0], near, right, left)
    sorted_cols = cols
    cols = trade(cols, ("y", "x"))

    pairs = n_rows * n_keys
    e, dp, st = call(
        functools.partial(scores_kernel, lat, heads),
        [((n_keys, n_rows), f32)] * 2 + [((4 * nx, rows), f32)], 5 + nx, smem=(0,),
        unused=(3,),
        flops=2 * pairs * (width + lat), moved=8 * pairs,
    )(pos, near, far, sorted_cols, *blocks)
    (stats,) = call(copies_kernel, [((nx,) + st.shape, f32)], 2, unused=(1,))(st, cols)
    stats = trade(stats, "x")
    p, ds, rope_part = call(
        functools.partial(dscores_kernel, lat),
        [((n_keys, n_rows), bf16)] * 2 + [((nz * ny, k_dev // 2, 2 * rope), bf16)],
        6 + nx, smem=(0,),
        flops=2 * pairs * rope, moved=12 * pairs,
    )(pos, stats, st, e, dp, *blocks)
    rope_part = trade(rope_part, ("z", "y"))

    mine, other, *dq = call(
        functools.partial(grads_kernel, lat),
        [((nz, k_dev, lat), bf16)] * 2 + [((rows, width), f32)] + [((rows, width), bf16)] * (nx - 1),
        5 + nx, flops=2 * pairs * (width + 2 * lat), moved=4 * pairs,
    )(p, ds, near, far, *blocks)
    other = lax.ppermute(other, "y", [(0, 1), (1, 0)])
    dq = [dq[0]] + [fetch(dq[k], nx - k, nx) for k in range(1, nx)]

    rope_all, rope_sum = call(
        rope_kernel, [((ny * nx, k_dev // 2, 2 * rope), bf16), ((k_dev, rope), f32)], 1
    )(rope_part)
    rope_all = trade(rope_all, ("y", "x"))
    (terms,) = call(
        weight_kernel, [((nd * nz, SLOT // 2, 2 * rope), f32)], 2,
        flops=2 * ny * nx * k_dev * wide * rope, moved=2 * ny * nx * k_dev * wide,
    )(cols, rope_all)
    terms = trade(terms, ("dp", "z"))
    (dweight,) = call(weight_sum_kernel, [((block, rope), f32)], 1)(terms)

    half = (mine.astype(f32) + other.astype(f32)).astype(bf16)
    half = trade(half, "z")
    (dlatent,) = call(latent_sum_kernel, [((k_dev, width), f32)], 2)(half, rope_sum)

    total = dq[0]
    for part in dq[1:]:
        total = total + part.astype(f32)
    return total.astype(bf16).reshape(query.shape), dlatent[None], dweight


def solution(mesh):
    fine = Mesh(mesh.devices.reshape(8, 8, 2, 4), ("dp", "z", "y", "x"))
    sp = ("z", "y", "x")
    in_specs = (
        P("dp", sp, None, None),
        P("dp", sp, None),
        P("dp", sp, None, None),
        P("dp", sp, None),
    )
    out_specs = (P("dp", sp, None, None), P("dp", sp, None), P(("dp",) + sp, None))
    return jax.shard_map(body, mesh=fine, in_specs=in_specs, out_specs=out_specs, check_vma=False)
```

```python
import functools

import jax
import jax.numpy as jnp
from jax import lax
from jax.experimental import pallas as pl
from jax.experimental.pallas import tpu as pltpu
from jax.sharding import Mesh, PartitionSpec as P

softmax_scale = 0.07216878364870323
f32, bf16 = jnp.float32, jnp.bfloat16
TILE = 256
SLOT = 16


def nt(a, b):
    return lax.dot_general(a, b, (((1,), (1,)), ((), ())), preferred_element_type=f32)


def nn(a, b):
    return lax.dot_general(a, b, (((1,), (0,)), ((), ())), preferred_element_type=f32)


def tn(a, b):
    return lax.dot_general(a, b, (((0,), (0,)), ((), ())), preferred_element_type=f32)


def call(kernel, outs, n_in, smem=(), unused=(), flops=0, moved=0, limit=48):
    vmem = pl.BlockSpec(memory_space=pltpu.VMEM)
    specs = [
        pl.BlockSpec(memory_space=pltpu.SMEM)
        if i in smem
        else (pl.BlockSpec(memory_space=pl.ANY) if i in unused else vmem)
        for i in range(n_in)
    ]
    return pl.pallas_call(
        kernel,
        out_shape=[jax.ShapeDtypeStruct(s, d) for s, d in outs],
        in_specs=specs,
        out_specs=[vmem] * len(outs),
        compiler_params=pltpu.CompilerParams(vmem_limit_bytes=limit * 2**20),
        cost_estimate=pl.CostEstimate(flops=flops, bytes_accessed=moved, transcendentals=0),
    )


def pack_kernel(dout, query, out):
    lat = dout.shape[1]
    width = query.shape[1]
    out[:, :lat] = dout[...]
    out[:, lat : lat + width] = query[...]
    out[:, lat + width :] = jnp.zeros((out.shape[0], out.shape[1] - lat - width), out.dtype)


def row_blocks(refs):
    own, right, first, second, left = refs
    return [
        lambda c: own[:, c],
        lambda c: right[:, c],
        lambda c: jnp.concatenate([first[:, c], second[:, c]]),
        lambda c: left[:, c],
    ]


def columns_kernel(block, n_z, n_grp, n_core, hid, out):
    k_dev, model = hid.shape
    n_data = model // (n_z * n_grp * block)
    span = n_z * n_grp * block
    wide = n_z * SLOT
    c = lax.broadcasted_iota(jnp.int32, (span, n_grp * wide), 0)
    o = lax.broadcasted_iota(jnp.int32, (span, n_grp * wide), 1)
    g, zz, k = o // wide, (o % wide) // SLOT, o % SLOT
    pick = jnp.where((c == (zz * n_grp + g) * block + k) & (k < block), 1.0, 0.0).astype(bf16)
    stacked = jnp.concatenate([hid[:, d * span : (d + 1) * span] for d in range(n_data)])
    moved = nn(stacked, pick).astype(bf16)
    for d in range(n_data):
        first = d // n_core * wide
        for g in range(n_grp):
            out[d % n_core * n_grp + g, :, first : first + wide] = moved[
                d * k_dev : (d + 1) * k_dev, g * wide : (g + 1) * wide
            ]


def key_tile(near, far, i, per):
    ref, first = (near, i * per) if i * per < near.shape[0] else (far, i * per - near.shape[0])
    k = ref[first : first + per]
    return k.reshape(k.shape[0] * k.shape[1], k.shape[2])


def scores_kernel(lat, heads, pos, near, far, after, *refs):
    blocks, (e_ref, dp_ref, st_ref) = row_blocks(refs[:-3]), refs[-3:]
    z, y, x = pos[0], pos[1], pos[2]
    n_z, k_dev, _ = near.shape
    n_x = len(blocks)
    rows = refs[0].shape[0]
    n_keys = 2 * n_z * k_dev
    tiles = n_keys // TILE
    per = TILE // k_dev
    tok = rows // heads
    first_query = n_z * 2 * n_x * (k_dev - tok)
    for b, t in enumerate(blocks):
        q, o = t(slice(lat, lat + near.shape[2])), t(slice(0, lat))
        cols = slice(b * rows, (b + 1) * rows)
        lane = lax.broadcasted_iota(jnp.int32, (k_dev, rows), 1)
        q_pos = ((z * 2 + y) * n_x + lax.rem(x + b, n_x)) * tok + lane // heads + first_query
        top = None
        for i in range(tiles):
            s = nt(key_tile(near, far, i, per), q) * softmax_scale
            half, zz = divmod((i + 1) * per - 1, n_z)
            if zz == n_z - 1:
                side = y if half == 0 else 1 - y
                k_pos = ((zz * 2 + side) * n_x + x) * k_dev + lax.broadcasted_iota(
                    jnp.int32, (k_dev, rows), 0
                )
                last = jnp.where(k_pos <= q_pos, s[TILE - k_dev :], -jnp.inf)
                s = jnp.concatenate([s[: TILE - k_dev], last])
            e_ref[i * TILE : (i + 1) * TILE, cols] = s
            m = jnp.max(s, axis=0, keepdims=True)
            top = m if top is None else jnp.maximum(top, m)
        total = jnp.zeros_like(top)
        delta = jnp.zeros_like(top)
        for i in range(tiles):
            part = slice(i * TILE, (i + 1) * TILE)
            dp = nt(key_tile(near, far, i, per)[:, :lat], o)
            e = jnp.exp(e_ref[part, cols] - top)
            e_ref[part, cols] = e
            dp_ref[part, cols] = dp
            total += jnp.sum(e, axis=0, keepdims=True)
            delta += jnp.sum(e * dp, axis=0, keepdims=True)
        st_ref[4 * b : 4 * b + 4] = jnp.concatenate([top, total, delta, jnp.zeros_like(top)])


def dscores_kernel(lat, pos, stats, st, e_ref, dp_ref, *refs):
    blocks, (p_ref, ds_ref, rope_ref) = row_blocks(refs[:-3]), refs[-3:]
    y, x = pos[1], pos[2]
    n_x = len(blocks)
    rows = refs[0].shape[0]
    tiles = e_ref.shape[0] // TILE
    grp, half_keys, _ = rope_ref.shape
    k_dev = 2 * half_keys
    for b in range(n_x):
        cols = slice(b * rows, (b + 1) * rows)
        theirs = []
        for s in range(n_x):
            at = lax.rem(x + b + n_x - s, n_x)
            v = stats[s, 0:4]
            for j in range(1, n_x):
                v = jnp.where(at == j, stats[s, 4 * j : 4 * j + 4], v)
            theirs.append(v)
        top = functools.reduce(jnp.maximum, [v[0:1] for v in theirs])
        w = [jnp.exp(v[0:1] - top) for v in theirs]
        total = sum(v[1:2] * u for v, u in zip(theirs, w))
        delta = sum(v[2:3] * u for v, u in zip(theirs, w)) / total
        f = jnp.exp(st[4 * b : 4 * b + 1] - top) / total
        for i in range(tiles):
            part = slice(i * TILE, (i + 1) * TILE)
            p = e_ref[part, cols] * f
            p_ref[part, cols] = p.astype(bf16)
            ds_ref[part, cols] = (p * (dp_ref[part, cols] - delta)).astype(bf16)
    n_z = grp // 2
    for i in range(tiles):
        part = slice(i * TILE, (i + 1) * TILE)
        r = None
        for b, t in enumerate(blocks):
            q = t(slice(2 * lat, 2 * lat + rope_ref.shape[2] // 2))
            v = nn(ds_ref[part, b * rows : (b + 1) * rows], q)
            r = v if r is None else r + v
        r = (r * softmax_scale).astype(bf16)
        for j in range(TILE // k_dev):
            half, zz = divmod(i * (TILE // k_dev) + j, n_z)
            side = y if half == 0 else 1 - y
            k = r[j * k_dev : (j + 1) * k_dev]
            rope_ref[2 * zz + side] = jnp.concatenate([k[:half_keys], k[half_keys:]], axis=1)


def latent_kernel(lat, p_ref, ds_ref, *refs):
    blocks, outs = row_blocks(refs[:5]), refs[5:]
    n_z, k_dev, _ = outs[0].shape
    rows = refs[0].shape[0]
    per = TILE // k_dev
    for i in range(p_ref.shape[0] // TILE):
        part = slice(i * TILE, (i + 1) * TILE)
        v = None
        for b, t in enumerate(blocks):
            a = nn(ds_ref[part, b * rows : (b + 1) * rows], t(slice(lat, 2 * lat)))
            v = a if v is None else v + a
        v = v * softmax_scale
        for b, t in enumerate(blocks):
            v += nn(p_ref[part, b * rows : (b + 1) * rows], t(slice(0, lat)))
        out, first = outs[i * per // n_z], i * per % n_z
        out[first : first + per] = v.astype(bf16).reshape(per, k_dev, lat)


def query_kernel(ds_ref, near, far, after, *outs):
    rows = outs[0].shape[0]
    per = TILE // near.shape[1]
    for b, out in enumerate(outs):
        v = None
        for i in range(ds_ref.shape[0] // TILE):
            a = tn(
                ds_ref[i * TILE : (i + 1) * TILE, b * rows : (b + 1) * rows],
                key_tile(near, far, i, per),
            )
            v = a if v is None else v + a
        out[...] = (v * softmax_scale).astype(out.dtype)


def weight_kernel(parts, cols, after, rope_ref, out):
    v = jnp.sum(parts[...].astype(f32), axis=0)
    e = v.shape[1] // 2
    rope = jnp.concatenate([v[:, :e], v[:, e:]])
    rope_ref[...] = rope
    low = rope.astype(bf16)
    for i in range(cols.shape[0]):
        out[i] = tn(low, cols[i]).astype(bf16)


def weight_half_kernel(parts, out):
    v = jnp.sum(parts[...].astype(f32), axis=0)
    v = jnp.swapaxes(v, 0, 1)
    v = v.reshape(v.shape[0] // SLOT, SLOT, v.shape[1])
    out[...] = jnp.concatenate([v[:, : SLOT // 2], v[:, SLOT // 2 :]], axis=2)


def weight_sum_kernel(parts, out):
    v = jnp.sum(parts[...], axis=0)
    e = v.shape[1] // 2
    out[...] = jnp.concatenate([v[:, :e], v[:, e:]])[: out.shape[0]]


def latent_sum_kernel(parts, rope, out):
    lat = parts.shape[1]
    out[:, :lat] = parts[...].astype(f32)
    out[:, lat:] = rope[...]


def fetch(value, offset, n):
    return lax.ppermute(value, "x", [(s, (s - offset) % n) for s in range(n)])


def trade(value, axes):
    return lax.all_to_all(value, axes, 0, 0, tiled=True)


def body(query, latent, dout, hidden):
    nw, nc, nz, ny, nx = (lax.axis_size(a) for a in ("w", "c", "z", "y", "x"))
    tok, heads, width = query.shape[1:]
    lat = dout.shape[3]
    rope = width - lat
    k_dev, model = hidden.shape[1:]
    rows = tok * heads
    n_rows, n_keys = nx * rows, nz * ny * k_dev
    pairs = n_rows * n_keys
    block = model // (nw * nc * nz * ny * nx)
    swap = [(0, 1), (1, 0)]
    pos = jnp.stack([lax.axis_index(a) for a in ("z", "y", "x")]).astype(jnp.int32)

    near = trade(jnp.broadcast_to(latent, (nz, k_dev, width)), "z")
    (own,) = call(pack_kernel, [((rows, -(-(lat + width) // 128) * 128), bf16)], 2, moved=4 * rows * width)(
        dout.reshape(rows, lat), query.reshape(rows, width)
    )
    right, left = fetch(own, 1, nx), fetch(own, nx - 1, nx)
    first, second = fetch(right[: rows // 2], 1, nx), fetch(left[rows // 2 :], nx - 1, nx)
    blocks = [own, right, first, second, left]
    far = lax.ppermute(near, "y", swap)

    wide = nw * nz * SLOT
    (cols,) = call(
        functools.partial(columns_kernel, block, nz, ny * nx, nc), [((nc * ny * nx, k_dev, wide), bf16)], 1,
        flops=2 * k_dev * model * 1024, moved=4 * k_dev * model, limit=20,
    )(hidden[0])
    e, dp, st = call(
        functools.partial(scores_kernel, lat, heads),
        [((n_keys, n_rows), f32)] * 2 + [((4 * nx, rows), f32)], 9, smem=(0,),
        unused=(3,),
        flops=2 * pairs * (width + lat), moved=8 * pairs, limit=20,
    )(pos, near, far, cols, *blocks)
    stats = trade(jnp.broadcast_to(st[None], (nx,) + st.shape), "x")
    p, ds, rope_part = call(
        functools.partial(dscores_kernel, lat),
        [((n_keys, n_rows), bf16)] * 2 + [((nz * ny, k_dev // 2, 2 * rope), bf16)], 10, smem=(0,),
        flops=2 * pairs * rope, moved=12 * pairs, limit=20,
    )(pos, stats, st, e, dp, *blocks)
    rope_part = trade(rope_part, ("z", "y"))
    mine, other = call(
        functools.partial(latent_kernel, lat), [((nz, k_dev, lat), bf16)] * 2, 7,
        flops=4 * pairs * lat, moved=4 * pairs, limit=20,
    )(p, ds, *blocks)
    other = lax.ppermute(other, "y", swap)
    rope_sum, terms = call(
        weight_kernel, [((k_dev, rope), f32), ((nc * ny * nx, rope, wide), bf16)], 3, unused=(2,),
        flops=2 * k_dev * nc * ny * nx * wide * rope, moved=4 * k_dev * model, limit=20,
    )(rope_part, cols, mine)
    after = terms
    terms = trade(terms, ("c", "y", "x"))
    dq = call(
        query_kernel, [((rows, width), f32)] + [((rows, width), bf16)] * (nx - 1), 4, unused=(3,),
        flops=2 * pairs * width, moved=4 * pairs, limit=20,
    )(ds, near, far, after)
    dq = [dq[0]] + [fetch(dq[k], nx - k, nx) for k in range(1, nx)]
    half = (mine.astype(f32) + other.astype(f32)).astype(bf16)
    half = lax.psum_scatter(half.reshape(nz * k_dev, lat), "z", scatter_dimension=0, tiled=True)
    (terms,) = call(weight_half_kernel, [((nw * nz, SLOT // 2, 2 * rope), f32)], 1, limit=20)(terms)
    terms = trade(terms, ("w", "z"))
    (dweight,) = call(weight_sum_kernel, [((block, rope), f32)], 1, limit=20)(terms)
    (dlatent,) = call(latent_sum_kernel, [((k_dev, width), f32)], 2, limit=20)(half, rope_sum)

    total = dq[0]
    for part in dq[1:]:
        total = total + part.astype(f32)
    return total.astype(bf16).reshape(query.shape), dlatent[None], dweight


def solution(mesh):
    fine = Mesh(mesh.devices.reshape(4, 2, 8, 2, 4), ("w", "c", "z", "y", "x"))
    dp, sp = ("w", "c"), ("z", "y", "x")
    tokens = P(dp, sp, None, None)
    keys = P(dp, sp, None)
    return jax.shard_map(
        body,
        mesh=fine,
        in_specs=(tokens, keys, tokens, keys),
        out_specs=(tokens, keys, P(dp + sp, None)),
        check_vma=False,
    )
```

```python
import functools

import jax
import jax.numpy as jnp
from jax import lax
from jax.experimental import pallas as pl
from jax.experimental.pallas import tpu as pltpu
from jax.sharding import Mesh, PartitionSpec as P

softmax_scale = 0.07216878364870323
f32, bf16 = jnp.float32, jnp.bfloat16
TILE = 256
SLOT = 16


def nt(a, b):
    return lax.dot_general(a, b, (((1,), (1,)), ((), ())), preferred_element_type=f32)


def nn(a, b):
    return lax.dot_general(a, b, (((1,), (0,)), ((), ())), preferred_element_type=f32)


def tn(a, b):
    return lax.dot_general(a, b, (((0,), (0,)), ((), ())), preferred_element_type=f32)


def call(kernel, outs, n_in, smem=(), unused=(), scratch=(), flops=0, moved=0, limit=20):
    vmem = pl.BlockSpec(memory_space=pltpu.VMEM)
    specs = [
        pl.BlockSpec(memory_space=pltpu.SMEM)
        if i in smem
        else (pl.BlockSpec(memory_space=pl.ANY) if i in unused else vmem)
        for i in range(n_in)
    ]
    return pl.pallas_call(
        kernel,
        out_shape=[jax.ShapeDtypeStruct(s, d) for s, d in outs],
        in_specs=specs,
        out_specs=[vmem] * len(outs),
        scratch_shapes=scratch,
        compiler_params=pltpu.CompilerParams(vmem_limit_bytes=limit * 2**20),
        cost_estimate=pl.CostEstimate(flops=flops, bytes_accessed=moved, transcendentals=0),
    )


def pack_kernel(dout, query, out):
    lat = dout.shape[1]
    width = query.shape[1]
    out[:, :lat] = dout[...]
    out[:, lat : lat + width] = query[...]
    out[:, lat + width :] = jnp.zeros((out.shape[0], out.shape[1] - lat - width), out.dtype)


def columns_kernel(block, n_z, n_grp, n_core, hid, out):
    k_dev, model = hid.shape
    n_data = model // (n_z * n_grp * block)
    span = n_z * n_grp * block
    wide = n_z * SLOT
    c = lax.broadcasted_iota(jnp.int32, (span, n_grp * wide), 0)
    o = lax.broadcasted_iota(jnp.int32, (span, n_grp * wide), 1)
    g, zz, k = o // wide, (o % wide) // SLOT, o % SLOT
    pick = jnp.where((c == (zz * n_grp + g) * block + k) & (k < block), 1.0, 0.0).astype(bf16)
    stacked = jnp.concatenate([hid[:, d * span : (d + 1) * span] for d in range(n_data)])
    moved = nn(stacked, pick).astype(bf16)
    for d in range(n_data):
        first = d // n_core * wide
        for g in range(n_grp):
            out[d % n_core * n_grp + g, :, first : first + wide] = moved[
                d * k_dev : (d + 1) * k_dev, g * wide : (g + 1) * wide
            ]


def key_tile(near, far, i, per):
    ref, first = (near, i * per) if i * per < near.shape[0] else (far, i * per - near.shape[0])
    k = ref[first : first + per]
    return k.reshape(k.shape[0] * k.shape[1], k.shape[2])


def scores_kernel(lat, heads, pos, near, far, after, *refs):
    blocks, (e_ref, dp_ref, st_ref) = refs[:-3], refs[-3:]
    z, y, x = pos[0], pos[1], pos[2]
    n_z, k_dev, _ = near.shape
    n_x = len(blocks)
    rows = refs[0].shape[0]
    n_keys = 2 * n_z * k_dev
    tiles = n_keys // TILE
    per = TILE // k_dev
    tok = rows // heads
    first_query = n_z * 2 * n_x * (k_dev - tok)
    for b, t in enumerate(blocks):
        q, o = t[:, lat : lat + near.shape[2]], t[:, :lat]
        cols = slice(b * rows, (b + 1) * rows)
        lane = lax.broadcasted_iota(jnp.int32, (k_dev, rows), 1)
        q_pos = ((z * 2 + y) * n_x + lax.rem(x + b, n_x)) * tok + lane // heads + first_query
        top = None
        for i in range(tiles):
            s = nt(key_tile(near, far, i, per), q) * softmax_scale
            half, zz = divmod((i + 1) * per - 1, n_z)
            if zz == n_z - 1:
                side = y if half == 0 else 1 - y
                k_pos = ((zz * 2 + side) * n_x + x) * k_dev + lax.broadcasted_iota(
                    jnp.int32, (k_dev, rows), 0
                )
                last = jnp.where(k_pos <= q_pos, s[TILE - k_dev :], -jnp.inf)
                s = jnp.concatenate([s[: TILE - k_dev], last])
            e_ref[i * TILE : (i + 1) * TILE, cols] = s
            m = jnp.max(s, axis=0, keepdims=True)
            top = m if top is None else jnp.maximum(top, m)
        total = jnp.zeros_like(top)
        delta = jnp.zeros_like(top)
        for i in range(tiles):
            part = slice(i * TILE, (i + 1) * TILE)
            dp = nt(key_tile(near, far, i, per)[:, :lat], o)
            e = jnp.exp(e_ref[part, cols] - top)
            e_ref[part, cols] = e
            dp_ref[part, cols] = dp
            total += jnp.sum(e, axis=0, keepdims=True)
            delta += jnp.sum(e * dp, axis=0, keepdims=True)
        st_ref[4 * b : 4 * b + 4] = jnp.concatenate([top, total, delta, jnp.zeros_like(top)])


def dscores_kernel(lat, pos, stats, st, e_ref, dp_ref, *refs):
    blocks, (ds_ref, rope_ref, mine, other, p_ref) = refs[:-5], refs[-5:]
    y, x = pos[1], pos[2]
    n_x = len(blocks)
    rows = refs[0].shape[0]
    tiles = e_ref.shape[0] // TILE
    grp, half_keys, _ = rope_ref.shape
    k_dev = 2 * half_keys
    for b in range(n_x):
        cols = slice(b * rows, (b + 1) * rows)
        theirs = []
        for s in range(n_x):
            at = lax.rem(x + b + n_x - s, n_x)
            v = stats[s, 0:4]
            for j in range(1, n_x):
                v = jnp.where(at == j, stats[s, 4 * j : 4 * j + 4], v)
            theirs.append(v)
        top = functools.reduce(jnp.maximum, [v[0:1] for v in theirs])
        w = [jnp.exp(v[0:1] - top) for v in theirs]
        total = sum(v[1:2] * u for v, u in zip(theirs, w))
        delta = sum(v[2:3] * u for v, u in zip(theirs, w)) / total
        f = jnp.exp(st[4 * b : 4 * b + 1] - top) / total
        for i in range(tiles):
            part = slice(i * TILE, (i + 1) * TILE)
            p = e_ref[part, cols] * f
            p_ref[part, cols] = p.astype(bf16)
            ds_ref[part, cols] = (p * (dp_ref[part, cols] - delta)).astype(bf16)
    n_z = grp // 2
    for i in range(tiles):
        part = slice(i * TILE, (i + 1) * TILE)
        r = None
        for b, t in enumerate(blocks):
            q = t[:, 2 * lat : 2 * lat + rope_ref.shape[2] // 2]
            v = nn(ds_ref[part, b * rows : (b + 1) * rows], q)
            r = v if r is None else r + v
        r = (r * softmax_scale).astype(bf16)
        for j in range(TILE // k_dev):
            half, zz = divmod(i * (TILE // k_dev) + j, n_z)
            side = y if half == 0 else 1 - y
            k = r[j * k_dev : (j + 1) * k_dev]
            rope_ref[2 * zz + side] = jnp.concatenate([k[:half_keys], k[half_keys:]], axis=1)
    per = TILE // k_dev
    for i in range(tiles):
        part = slice(i * TILE, (i + 1) * TILE)
        v = None
        for b, t in enumerate(blocks):
            a = nn(ds_ref[part, b * rows : (b + 1) * rows], t[:, lat : 2 * lat])
            v = a if v is None else v + a
        v = v * softmax_scale
        for b, t in enumerate(blocks):
            v += nn(p_ref[part, b * rows : (b + 1) * rows], t[:, :lat])
        out, first = (mine, other)[i * per // n_z], i * per % n_z
        out[first : first + per] = v.astype(bf16).reshape(per, k_dev, lat)


def query_kernel(ds_ref, near, far, after, *outs):
    rows = outs[0].shape[0]
    per = TILE // near.shape[1]
    for b, out in enumerate(outs):
        v = None
        for i in range(ds_ref.shape[0] // TILE):
            a = tn(
                ds_ref[i * TILE : (i + 1) * TILE, b * rows : (b + 1) * rows],
                key_tile(near, far, i, per),
            )
            v = a if v is None else v + a
        out[...] = (v * softmax_scale).astype(out.dtype)


def weight_kernel(parts, cols, after, rope_ref, out):
    v = jnp.sum(parts[...].astype(f32), axis=0)
    e = v.shape[1] // 2
    rope = jnp.concatenate([v[:, :e], v[:, e:]])
    rope_ref[...] = rope
    low = rope.astype(bf16)
    for i in range(cols.shape[0]):
        out[i] = tn(low, cols[i]).astype(bf16)


def weight_half_kernel(parts, after, after2, out):
    v = jnp.sum(parts[...].astype(f32), axis=0)
    v = jnp.swapaxes(v, 0, 1)
    v = v.reshape(v.shape[0] // SLOT, SLOT, v.shape[1])
    out[...] = jnp.concatenate([v[:, : SLOT // 2], v[:, SLOT // 2 :]], axis=2)


def weight_sum_kernel(parts, out):
    v = jnp.sum(parts[...], axis=0)
    e = v.shape[1] // 2
    out[...] = jnp.concatenate([v[:, :e], v[:, e:]])[: out.shape[0]]


def halve_kernel(bit, pos, a, b, after, *refs):
    keep, send = refs[-2:]
    mine = (pos[0] >> bit) & 1
    for i in range(keep.shape[0]):
        at, away = 2 * i + mine, 2 * i + 1 - mine
        keep[i] = a[at].astype(f32) + b[at].astype(f32)
        send[i] = (a[away].astype(f32) + b[away].astype(f32)).astype(send.dtype)


def latent_sum_kernel(a, b, rope, out):
    lat = a.shape[2]
    out[:, :lat] = a[0] + b[0].astype(f32)
    out[:, lat:] = rope[...]


def fetch(value, offset, n):
    return lax.ppermute(value, "x", [(s, (s - offset) % n) for s in range(n)])


def trade(value, axes):
    return lax.all_to_all(value, axes, 0, 0, tiled=True)


def body(query, latent, dout, hidden):
    nw, nc, nz, ny, nx = (lax.axis_size(a) for a in ("w", "c", "z", "y", "x"))
    tok, heads, width = query.shape[1:]
    lat = dout.shape[3]
    rope = width - lat
    k_dev, model = hidden.shape[1:]
    rows = tok * heads
    n_rows, n_keys = nx * rows, nz * ny * k_dev
    pairs = n_rows * n_keys
    block = model // (nw * nc * nz * ny * nx)
    swap = [(0, 1), (1, 0)]
    pos = jnp.stack([lax.axis_index(a) for a in ("z", "y", "x")]).astype(jnp.int32)

    near = trade(jnp.broadcast_to(latent, (nz, k_dev, width)), "z")
    (own,) = call(pack_kernel, [((rows, -(-(lat + width) // 128) * 128), bf16)], 2, moved=4 * rows * width)(
        dout.reshape(rows, lat), query.reshape(rows, width)
    )
    blocks = [own] + [fetch(own, k, nx) for k in range(1, nx)]
    far = lax.ppermute(near, "y", swap)

    wide = nw * nz * SLOT
    (cols,) = call(
        functools.partial(columns_kernel, block, nz, ny * nx, nc), [((nc * ny * nx, k_dev, wide), bf16)], 1,
        flops=2 * k_dev * model * 1024, moved=4 * k_dev * model, limit=20,
    )(hidden[0])
    e, dp, st = call(
        functools.partial(scores_kernel, lat, heads),
        [((n_keys, n_rows), f32)] * 2 + [((4 * nx, rows), f32)], 8, smem=(0,),
        unused=(3,),
        flops=2 * pairs * (width + lat), moved=8 * pairs, limit=20,
    )(pos, near, far, cols, *blocks)
    stats = trade(jnp.broadcast_to(st[None], (nx,) + st.shape), "x")
    ds, rope_part, mine, other = call(
        functools.partial(dscores_kernel, lat),
        [((n_keys, n_rows), bf16), ((nz * ny, k_dev // 2, 2 * rope), bf16)] + [((nz, k_dev, lat), bf16)] * 2,
        9, smem=(0,), scratch=[pltpu.VMEM((n_keys, n_rows), bf16)],
        flops=2 * pairs * (rope + 2 * lat), moved=12 * pairs,
    )(pos, stats, st, e, dp, *blocks)
    rope_part = trade(rope_part, ("z", "y"))
    other = lax.ppermute(other, "y", swap)
    rope_sum, terms = call(
        weight_kernel, [((k_dev, rope), f32), ((nc * ny * nx, rope, wide), bf16)], 3, unused=(2,),
        flops=2 * k_dev * nc * ny * nx * wide * rope, moved=4 * k_dev * model, limit=20,
    )(rope_part, cols, other)
    after = terms
    terms = trade(terms, ("c", "y", "x"))
    dq = call(
        query_kernel, [((rows, width), f32)] + [((rows, width), bf16)] * (nx - 1), 4, unused=(3,),
        flops=2 * pairs * width, moved=4 * pairs, limit=20,
    )(ds, near, far, after)
    query_part = dq[1]
    dq = [dq[0]] + [fetch(dq[k], nx - k, nx) for k in range(1, nx)]
    kept, came = mine, other
    for bit in range(3):
        if bit == 2:
            (terms,) = call(
                weight_half_kernel, [((nw * nz, SLOT // 2, 2 * rope), f32)], 3, unused=(1, 2)
            )(terms, kept, query_part)
            after = terms
            terms = trade(terms, ("w", "z"))
        n = nz >> (bit + 1)
        kept, sent = call(
            functools.partial(halve_kernel, bit), [((n, k_dev, lat), f32), ((n, k_dev, lat), bf16)], 4,
            smem=(0,), unused=(3,), flops=8 * n * k_dev * lat, moved=12 * n * k_dev * lat, limit=20,
        )(pos, kept, came, after)
        came = lax.ppermute(sent, "z", [(i, i ^ (1 << bit)) for i in range(nz)])
    (dweight,) = call(weight_sum_kernel, [((block, rope), f32)], 1)(terms)
    (dlatent,) = call(latent_sum_kernel, [((k_dev, width), f32)], 3)(kept, came, rope_sum)

    total = dq[0]
    for part in dq[1:]:
        total = total + part.astype(f32)
    return total.astype(bf16).reshape(query.shape), dlatent[None], dweight


def solution(mesh):
    fine = Mesh(mesh.devices.reshape(4, 2, 8, 2, 4), ("w", "c", "z", "y", "x"))
    dp, sp = ("w", "c"), ("z", "y", "x")
    tokens = P(dp, sp, None, None)
    keys = P(dp, sp, None)
    return jax.shard_map(
        body,
        mesh=fine,
        in_specs=(tokens, keys, tokens, keys),
        out_specs=(tokens, keys, P(dp + sp, None)),
        check_vma=False,
    )
```

```python
import functools

import jax
import jax.numpy as jnp
from jax import lax
from jax.experimental import pallas as pl
from jax.experimental.pallas import tpu as pltpu
from jax.sharding import Mesh, PartitionSpec as P

softmax_scale = 0.07216878364870323
f32, bf16 = jnp.float32, jnp.bfloat16
TILE = 256
SLOT = 16


def nt(a, b):
    return lax.dot_general(a, b, (((1,), (1,)), ((), ())), preferred_element_type=f32)


def nn(a, b):
    return lax.dot_general(a, b, (((1,), (0,)), ((), ())), preferred_element_type=f32)


def tn(a, b):
    return lax.dot_general(a, b, (((0,), (0,)), ((), ())), preferred_element_type=f32)


def call(kernel, outs, n_in, smem=(), unused=(), scratch=(), flops=0, moved=0, limit=20):
    vmem = pl.BlockSpec(memory_space=pltpu.VMEM)
    specs = [
        pl.BlockSpec(memory_space=pltpu.SMEM)
        if i in smem
        else (pl.BlockSpec(memory_space=pl.ANY) if i in unused else vmem)
        for i in range(n_in)
    ]
    return pl.pallas_call(
        kernel,
        out_shape=[jax.ShapeDtypeStruct(s, d) for s, d in outs],
        in_specs=specs,
        out_specs=[vmem] * len(outs),
        scratch_shapes=scratch,
        compiler_params=pltpu.CompilerParams(vmem_limit_bytes=limit * 2**20),
        cost_estimate=pl.CostEstimate(flops=flops, bytes_accessed=moved, transcendentals=0),
    )


def pack_kernel(dout, query, out):
    lat = dout.shape[1]
    width = query.shape[1]
    out[:, :lat] = dout[...]
    out[:, lat : lat + width] = query[...]
    out[:, lat + width :] = jnp.zeros((out.shape[0], out.shape[1] - lat - width), out.dtype)


def columns_kernel(block, n_z, n_grp, n_core, hid, out):
    k_dev, model = hid.shape
    n_data = model // (n_z * n_grp * block)
    span = n_z * n_grp * block
    wide = n_z * SLOT
    c = lax.broadcasted_iota(jnp.int32, (span, n_grp * wide), 0)
    o = lax.broadcasted_iota(jnp.int32, (span, n_grp * wide), 1)
    g, zz, k = o // wide, (o % wide) // SLOT, o % SLOT
    pick = jnp.where((c == (zz * n_grp + g) * block + k) & (k < block), 1.0, 0.0).astype(bf16)
    stacked = jnp.concatenate([hid[:, d * span : (d + 1) * span] for d in range(n_data)])
    moved = nn(stacked, pick).astype(bf16)
    for d in range(n_data):
        first = d // n_core * wide
        for g in range(n_grp):
            out[d % n_core * n_grp + g, :, first : first + wide] = moved[
                d * k_dev : (d + 1) * k_dev, g * wide : (g + 1) * wide
            ]


def key_tile(keys, i, per):
    k = keys[i * per : (i + 1) * per]
    return k.reshape(k.shape[0] * k.shape[1], k.shape[2])


def scores_kernel(lat, heads, pos, keys, after, *refs):
    blocks, (e_ref, dp_ref, st_ref) = refs[:-3], refs[-3:]
    z, y, x = pos[0], pos[1], pos[2]
    grp, k_dev, width = keys.shape
    n_x = len(blocks)
    rows = refs[0].shape[0]
    n_keys = grp * k_dev
    tiles = n_keys // TILE
    per = TILE // k_dev
    tok = rows // heads
    first_query = grp * n_x * (k_dev - tok)
    for b, t in enumerate(blocks):
        q, o = t[:, lat : lat + width], t[:, :lat]
        cols = slice(b * rows, (b + 1) * rows)
        lane = lax.broadcasted_iota(jnp.int32, (k_dev, rows), 1)
        q_pos = ((z * 2 + y) * n_x + lax.rem(x + b, n_x)) * tok + lane // heads + first_query
        top = None
        for i in range(tiles):
            s = nt(key_tile(keys, i, per), q) * softmax_scale
            if i == tiles - 1:
                k_pos = ((grp - 1) * n_x + x) * k_dev + lax.broadcasted_iota(
                    jnp.int32, (k_dev, rows), 0
                )
                last = jnp.where(k_pos <= q_pos, s[TILE - k_dev :], -jnp.inf)
                s = jnp.concatenate([s[: TILE - k_dev], last])
            e_ref[i * TILE : (i + 1) * TILE, cols] = s
            m = jnp.max(s, axis=0, keepdims=True)
            top = m if top is None else jnp.maximum(top, m)
        total = jnp.zeros_like(top)
        delta = jnp.zeros_like(top)
        for i in range(tiles):
            part = slice(i * TILE, (i + 1) * TILE)
            dp = nt(key_tile(keys, i, per)[:, :lat], o)
            e = jnp.exp(e_ref[part, cols] - top)
            e_ref[part, cols] = e
            dp_ref[part, cols] = dp
            total += jnp.sum(e, axis=0, keepdims=True)
            delta += jnp.sum(e * dp, axis=0, keepdims=True)
        st_ref[4 * b : 4 * b + 4] = jnp.concatenate([top, total, delta, jnp.zeros_like(top)])


def dscores_kernel(lat, pos, stats, st, e_ref, dp_ref, *refs):
    blocks, (ds_ref, rope_ref, mine, other, p_ref) = refs[:-5], refs[-5:]
    y, x = pos[1], pos[2]
    n_x = len(blocks)
    rows = refs[0].shape[0]
    tiles = e_ref.shape[0] // TILE
    grp, half_keys, _ = rope_ref.shape
    k_dev = 2 * half_keys
    for b in range(n_x):
        cols = slice(b * rows, (b + 1) * rows)
        theirs = []
        for s in range(n_x):
            at = lax.rem(x + b + n_x - s, n_x)
            v = stats[s, 0:4]
            for j in range(1, n_x):
                v = jnp.where(at == j, stats[s, 4 * j : 4 * j + 4], v)
            theirs.append(v)
        top = functools.reduce(jnp.maximum, [v[0:1] for v in theirs])
        w = [jnp.exp(v[0:1] - top) for v in theirs]
        total = sum(v[1:2] * u for v, u in zip(theirs, w))
        delta = sum(v[2:3] * u for v, u in zip(theirs, w)) / total
        f = jnp.exp(st[4 * b : 4 * b + 1] - top) / total
        for i in range(tiles):
            part = slice(i * TILE, (i + 1) * TILE)
            p = e_ref[part, cols] * f
            p_ref[part, cols] = p.astype(bf16)
            ds_ref[part, cols] = (p * (dp_ref[part, cols] - delta)).astype(bf16)
    for i in range(tiles):
        part = slice(i * TILE, (i + 1) * TILE)
        r = None
        for b, t in enumerate(blocks):
            q = t[:, 2 * lat : 2 * lat + rope_ref.shape[2] // 2]
            v = nn(ds_ref[part, b * rows : (b + 1) * rows], q)
            r = v if r is None else r + v
        r = (r * softmax_scale).astype(bf16)
        for j in range(TILE // k_dev):
            k = r[j * k_dev : (j + 1) * k_dev]
            rope_ref[i * (TILE // k_dev) + j] = jnp.concatenate([k[:half_keys], k[half_keys:]], axis=1)
    per = TILE // k_dev
    for i in range(tiles):
        part = slice(i * TILE, (i + 1) * TILE)
        v = None
        for b, t in enumerate(blocks):
            a = nn(ds_ref[part, b * rows : (b + 1) * rows], t[:, lat : 2 * lat])
            v = a if v is None else v + a
        v = v * softmax_scale
        for b, t in enumerate(blocks):
            v += nn(p_ref[part, b * rows : (b + 1) * rows], t[:, :lat])
        v = v.astype(bf16).reshape(per // 2, 2, k_dev, lat)
        first = i * per // 2
        for out, side in ((mine, y), (other, 1 - y)):
            out[first : first + per // 2] = jnp.where(side == 0, v[:, 0], v[:, 1])


def query_kernel(ds_ref, keys, *outs):
    rows = outs[0].shape[0]
    per = TILE // keys.shape[1]
    for b, out in enumerate(outs):
        v = None
        for i in range(ds_ref.shape[0] // TILE):
            a = tn(
                ds_ref[i * TILE : (i + 1) * TILE, b * rows : (b + 1) * rows],
                key_tile(keys, i, per),
            )
            v = a if v is None else v + a
        out[...] = (v * softmax_scale).astype(out.dtype)


def weight_kernel(parts, cols, after, after2, rope_ref, out):
    v = jnp.sum(parts[...].astype(f32), axis=0)
    e = v.shape[1] // 2
    rope = jnp.concatenate([v[:, :e], v[:, e:]])
    rope_ref[...] = rope
    low = rope.astype(bf16)
    for i in range(cols.shape[0]):
        out[i] = tn(low, cols[i]).astype(bf16)


def weight_half_kernel(parts, after, out):
    v = jnp.sum(parts[...].astype(f32), axis=0)
    v = jnp.swapaxes(v, 0, 1)
    v = v.reshape(v.shape[0] // SLOT, SLOT, v.shape[1])
    out[...] = jnp.concatenate([v[:, : SLOT // 2], v[:, SLOT // 2 :]], axis=2)


def weight_sum_kernel(parts, out):
    v = jnp.sum(parts[...], axis=0)
    e = v.shape[1] // 2
    out[...] = jnp.concatenate([v[:, :e], v[:, e:]])[: out.shape[0]]


def halve_kernel(bit, pos, a, b, after, *refs):
    keep, send = refs[-2:]
    mine = (pos[0] >> bit) & 1
    for i in range(keep.shape[0]):
        at, away = 2 * i + mine, 2 * i + 1 - mine
        keep[i] = a[at].astype(f32) + b[at].astype(f32)
        send[i] = (a[away].astype(f32) + b[away].astype(f32)).astype(send.dtype)


def latent_sum_kernel(a, b, rope, out):
    lat = a.shape[2]
    out[:, :lat] = a[0] + b[0].astype(f32)
    out[:, lat:] = rope[...]


def fetch(value, offset, n):
    return lax.ppermute(value, "x", [(s, (s - offset) % n) for s in range(n)])


def trade(value, axes):
    return lax.all_to_all(value, axes, 0, 0, tiled=True)


def body(query, latent, dout, hidden):
    nw, nc, nz, ny, nx = (lax.axis_size(a) for a in ("w", "c", "z", "y", "x"))
    tok, heads, width = query.shape[1:]
    lat = dout.shape[3]
    rope = width - lat
    k_dev, model = hidden.shape[1:]
    rows = tok * heads
    n_rows, n_keys = nx * rows, nz * ny * k_dev
    pairs = n_rows * n_keys
    block = model // (nw * nc * nz * ny * nx)
    swap = [(0, 1), (1, 0)]
    pos = jnp.stack([lax.axis_index(a) for a in ("z", "y", "x")]).astype(jnp.int32)

    keys = trade(jnp.broadcast_to(latent, (nz * ny, k_dev, width)), ("z", "y"))
    (own,) = call(pack_kernel, [((rows, -(-(lat + width) // 128) * 128), bf16)], 2, moved=4 * rows * width)(
        dout.reshape(rows, lat), query.reshape(rows, width)
    )
    blocks = [own] + [fetch(own, k, nx) for k in range(1, nx)]

    wide = nw * nz * SLOT
    (cols,) = call(
        functools.partial(columns_kernel, block, nz, ny * nx, nc), [((nc * ny * nx, k_dev, wide), bf16)], 1,
        flops=2 * k_dev * model * 1024, moved=4 * k_dev * model, limit=20,
    )(hidden[0])
    e, dp, st = call(
        functools.partial(scores_kernel, lat, heads),
        [((n_keys, n_rows), f32)] * 2 + [((4 * nx, rows), f32)], 7, smem=(0,),
        unused=(2,),
        flops=2 * pairs * (width + lat), moved=8 * pairs, limit=20,
    )(pos, keys, cols, *blocks)
    stats = trade(jnp.broadcast_to(st[None], (nx,) + st.shape), "x")
    ds, rope_part, mine, other = call(
        functools.partial(dscores_kernel, lat),
        [((n_keys, n_rows), bf16), ((nz * ny, k_dev // 2, 2 * rope), bf16)] + [((nz, k_dev, lat), bf16)] * 2,
        9, smem=(0,), scratch=[pltpu.VMEM((n_keys, n_rows), bf16)],
        flops=2 * pairs * (rope + 2 * lat), moved=12 * pairs,
    )(pos, stats, st, e, dp, *blocks)
    rope_part = trade(rope_part, ("z", "y"))
    other = lax.ppermute(other, "y", swap)
    dq = call(
        query_kernel, [((rows, width), f32)] + [((rows, width), bf16)] * (nx - 1), 2,
        flops=2 * pairs * width, moved=4 * pairs,
    )(ds, keys)
    rope_sum, terms = call(
        weight_kernel, [((k_dev, rope), f32), ((nc * ny * nx, rope, wide), bf16)], 4, unused=(2, 3),
        flops=2 * k_dev * nc * ny * nx * wide * rope, moved=4 * k_dev * model, limit=20,
    )(rope_part, cols, other, dq[1])
    after = terms
    terms = trade(terms, ("c", "y", "x"))
    dq = [dq[0]] + [fetch(dq[k], nx - k, nx) for k in range(1, nx)]
    kept, came = mine, other
    for bit in range(3):
        if bit == 2:
            (terms,) = call(
                weight_half_kernel, [((nw * nz, SLOT // 2, 2 * rope), f32)], 2, unused=(1,)
            )(terms, kept)
            after = terms
            terms = trade(terms, ("w", "z"))
        n = nz >> (bit + 1)
        kept, sent = call(
            functools.partial(halve_kernel, bit), [((n, k_dev, lat), f32), ((n, k_dev, lat), bf16)], 4,
            smem=(0,), unused=(3,), flops=8 * n * k_dev * lat, moved=12 * n * k_dev * lat, limit=20,
        )(pos, kept, came, after)
        came = lax.ppermute(sent, "z", [(i, i ^ (1 << bit)) for i in range(nz)])
    (dweight,) = call(weight_sum_kernel, [((block, rope), f32)], 1)(terms)
    (dlatent,) = call(latent_sum_kernel, [((k_dev, width), f32)], 3)(kept, came, rope_sum)

    total = dq[0]
    for part in dq[1:]:
        total = total + part.astype(f32)
    return total.astype(bf16).reshape(query.shape), dlatent[None], dweight


def solution(mesh):
    fine = Mesh(mesh.devices.reshape(4, 2, 8, 2, 4), ("w", "c", "z", "y", "x"))
    dp, sp = ("w", "c"), ("z", "y", "x")
    tokens = P(dp, sp, None, None)
    keys = P(dp, sp, None)
    return jax.shard_map(
        body,
        mesh=fine,
        in_specs=(tokens, keys, tokens, keys),
        out_specs=(tokens, keys, P(dp + sp, None)),
        check_vma=False,
    )
```

```python
import functools

import jax
import jax.numpy as jnp
from jax import lax
from jax.experimental import pallas as pl
from jax.experimental.pallas import tpu as pltpu
from jax.sharding import Mesh, PartitionSpec as P

softmax_scale = 0.07216878364870323
f32, bf16 = jnp.float32, jnp.bfloat16
TILE = 256
TOKEN = ((8, 128), jnp.float32)
SLOT = 16


def nt(a, b):
    return lax.dot_general(a, b, (((1,), (1,)), ((), ())), preferred_element_type=f32)


def nn(a, b):
    return lax.dot_general(a, b, (((1,), (0,)), ((), ())), preferred_element_type=f32)


def tn(a, b):
    return lax.dot_general(a, b, (((0,), (0,)), ((), ())), preferred_element_type=f32)


def call(kernel, outs, n_in, smem=(), unused=(), scratch=(), flops=0, moved=0, limit=20):
    vmem = pl.BlockSpec(memory_space=pltpu.VMEM)
    specs = [
        pl.BlockSpec(memory_space=pltpu.SMEM)
        if i in smem
        else (pl.BlockSpec(memory_space=pl.ANY) if i in unused else vmem)
        for i in range(n_in)
    ]
    return pl.pallas_call(
        kernel,
        out_shape=[jax.ShapeDtypeStruct(s, d) for s, d in outs],
        in_specs=specs,
        out_specs=[vmem] * len(outs),
        scratch_shapes=scratch,
        compiler_params=pltpu.CompilerParams(vmem_limit_bytes=limit * 2**20),
        cost_estimate=pl.CostEstimate(flops=flops, bytes_accessed=moved, transcendentals=0),
    )


def pack_kernel(dout, query, out):
    lat = dout.shape[1]
    width = query.shape[1]
    out[:, :lat] = dout[...]
    out[:, lat : lat + width] = query[...]
    out[:, lat + width :] = jnp.zeros((out.shape[0], out.shape[1] - lat - width), out.dtype)


def columns_kernel(block, n_z, n_grp, n_core, hid, out, token):
    token[...] = jnp.zeros(token.shape, token.dtype)
    k_dev, model = hid.shape
    n_data = model // (n_z * n_grp * block)
    span = n_z * n_grp * block
    wide = n_z * SLOT
    c = lax.broadcasted_iota(jnp.int32, (span, n_grp * wide), 0)
    o = lax.broadcasted_iota(jnp.int32, (span, n_grp * wide), 1)
    g, zz, k = o // wide, (o % wide) // SLOT, o % SLOT
    pick = jnp.where((c == (zz * n_grp + g) * block + k) & (k < block), 1.0, 0.0).astype(bf16)
    stacked = jnp.concatenate([hid[:, d * span : (d + 1) * span] for d in range(n_data)])
    moved = nn(stacked, pick).astype(bf16)
    for d in range(n_data):
        first = d // n_core * wide
        for g in range(n_grp):
            out[d % n_core * n_grp + g, :, first : first + wide] = moved[
                d * k_dev : (d + 1) * k_dev, g * wide : (g + 1) * wide
            ]


def key_tile(keys, i, per):
    k = keys[i * per : (i + 1) * per]
    return k.reshape(k.shape[0] * k.shape[1], k.shape[2])


def scores_kernel(lat, heads, pos, keys, after, *refs):
    blocks, (e_ref, dp_ref, st_ref) = refs[:-3], refs[-3:]
    z, y, x = pos[0], pos[1], pos[2]
    grp, k_dev, width = keys.shape
    n_x = len(blocks)
    rows = refs[0].shape[0]
    n_keys = grp * k_dev
    tiles = n_keys // TILE
    per = TILE // k_dev
    tok = rows // heads
    first_query = grp * n_x * (k_dev - tok)
    for b, t in enumerate(blocks):
        q, o = t[:, lat : lat + width], t[:, :lat]
        cols = slice(b * rows, (b + 1) * rows)
        lane = lax.broadcasted_iota(jnp.int32, (k_dev, rows), 1)
        q_pos = ((z * 2 + y) * n_x + lax.rem(x + b, n_x)) * tok + lane // heads + first_query
        top = None
        for i in range(tiles):
            s = nt(key_tile(keys, i, per), q) * softmax_scale
            if i == tiles - 1:
                k_pos = ((grp - 1) * n_x + x) * k_dev + lax.broadcasted_iota(
                    jnp.int32, (k_dev, rows), 0
                )
                last = jnp.where(k_pos <= q_pos, s[TILE - k_dev :], -jnp.inf)
                s = jnp.concatenate([s[: TILE - k_dev], last])
            e_ref[i * TILE : (i + 1) * TILE, cols] = s
            m = jnp.max(s, axis=0, keepdims=True)
            top = m if top is None else jnp.maximum(top, m)
        total = jnp.zeros_like(top)
        delta = jnp.zeros_like(top)
        for i in range(tiles):
            part = slice(i * TILE, (i + 1) * TILE)
            dp = nt(key_tile(keys, i, per)[:, :lat], o)
            e = jnp.exp(e_ref[part, cols] - top)
            e_ref[part, cols] = e
            dp_ref[part, cols] = dp
            total += jnp.sum(e, axis=0, keepdims=True)
            delta += jnp.sum(e * dp, axis=0, keepdims=True)
        st_ref[4 * b : 4 * b + 4] = jnp.concatenate([top, total, delta, jnp.zeros_like(top)])


def dscores_kernel(lat, pos, stats, st, e_ref, dp_ref, *refs):
    n_x = stats.shape[0]
    blocks, (keys, rope_ref, mine, other) = refs[:n_x], refs[n_x : n_x + 4]
    own, keep, send, p_ref, ds_ref = refs[n_x + 4 :]
    y, x = pos[1], pos[2]
    rows = refs[0].shape[0]
    tiles = e_ref.shape[0] // TILE
    grp, half_keys, _ = rope_ref.shape
    k_dev = 2 * half_keys
    for b in range(n_x):
        cols = slice(b * rows, (b + 1) * rows)
        theirs = []
        for s in range(n_x):
            at = lax.rem(x + b + n_x - s, n_x)
            v = stats[s, 0:4]
            for j in range(1, n_x):
                v = jnp.where(at == j, stats[s, 4 * j : 4 * j + 4], v)
            theirs.append(v)
        top = functools.reduce(jnp.maximum, [v[0:1] for v in theirs])
        w = [jnp.exp(v[0:1] - top) for v in theirs]
        total = sum(v[1:2] * u for v, u in zip(theirs, w))
        delta = sum(v[2:3] * u for v, u in zip(theirs, w)) / total
        f = jnp.exp(st[4 * b : 4 * b + 1] - top) / total
        for i in range(tiles):
            part = slice(i * TILE, (i + 1) * TILE)
            p = e_ref[part, cols] * f
            p_ref[part, cols] = p.astype(bf16)
            ds_ref[part, cols] = (p * (dp_ref[part, cols] - delta)).astype(bf16)
    for i in range(tiles):
        part = slice(i * TILE, (i + 1) * TILE)
        r = None
        for b, t in enumerate(blocks):
            q = t[:, 2 * lat : 2 * lat + rope_ref.shape[2] // 2]
            v = nn(ds_ref[part, b * rows : (b + 1) * rows], q)
            r = v if r is None else r + v
        r = (r * softmax_scale).astype(bf16)
        for j in range(TILE // k_dev):
            k = r[j * k_dev : (j + 1) * k_dev]
            rope_ref[i * (TILE // k_dev) + j] = jnp.concatenate([k[:half_keys], k[half_keys:]], axis=1)
    per = TILE // k_dev
    for i in range(tiles):
        part = slice(i * TILE, (i + 1) * TILE)
        v = None
        for b, t in enumerate(blocks):
            a = nn(ds_ref[part, b * rows : (b + 1) * rows], t[:, lat : 2 * lat])
            v = a if v is None else v + a
        v = v * softmax_scale
        for b, t in enumerate(blocks):
            v += nn(p_ref[part, b * rows : (b + 1) * rows], t[:, :lat])
        v = v.astype(bf16).reshape(per // 2, 2, k_dev, lat)
        first = i * per // 2
        for out, side in ((mine, y), (other, 1 - y)):
            out[first : first + per // 2] = jnp.where(side == 0, v[:, 0], v[:, 1])
    dq = []
    for b in range(n_x):
        v = None
        for i in range(tiles):
            part = slice(i * TILE, (i + 1) * TILE)
            a = tn(ds_ref[part, b * rows : (b + 1) * rows], key_tile(keys, i, per))
            v = a if v is None else v + a
        dq.append(v * softmax_scale)
    own[...] = dq[0]
    even = lax.rem(x, 2) == 0
    keep[...] = jnp.where(even, dq[3], dq[1])
    send[...] = jnp.concatenate([jnp.where(even, dq[1], dq[3]), dq[2]], axis=1).astype(bf16)


def query_half_kernel(own, keep, came, own_out, send, token):
    token[...] = jnp.zeros(token.shape, token.dtype)
    width = own.shape[1]
    own_out[...] = own[...] + came[:, :width].astype(f32)
    send[...] = (keep[...] + came[:, width:].astype(f32)).astype(bf16)


def weight_kernel(parts, cols, after, after2, rope_ref, out):
    v = jnp.sum(parts[...].astype(f32), axis=0)
    e = v.shape[1] // 2
    rope = jnp.concatenate([v[:, :e], v[:, e:]])
    rope_ref[...] = rope
    low = rope.astype(bf16)
    for i in range(cols.shape[0]):
        out[i] = tn(low, cols[i]).astype(bf16)


def weight_half_kernel(parts, after, out, token):
    token[...] = jnp.zeros(token.shape, token.dtype)
    n_z = out.shape[0]
    half = SLOT // 2
    v = jnp.sum(parts[...].astype(f32), axis=0)
    v = jnp.swapaxes(v, 0, 1)
    v = v.reshape(v.shape[0] // SLOT, SLOT, v.shape[1])
    v = jnp.concatenate([v[:, :half], v[:, half:]], axis=2)
    for i in range(v.shape[0]):
        w = i // n_z
        out[i % n_z, w * half : (w + 1) * half] = v[i]


def weight_next_kernel(parts, out):
    v = jnp.sum(parts[...], axis=0)
    out[...] = v.reshape(out.shape)


def weight_sum_kernel(parts, out):
    v = jnp.sum(parts[...], axis=0)
    e = v.shape[1] // 2
    out[...] = jnp.concatenate([v[:, :e], v[:, e:]])[: out.shape[0]]


def halve_kernel(bit, pos, a, b, after, *refs):
    keep, send, token = refs
    token[...] = jnp.zeros(token.shape, token.dtype)
    mine = (pos[0] >> bit) & 1
    for i in range(keep.shape[0]):
        at, away = 2 * i + mine, 2 * i + 1 - mine
        keep[i] = a[at].astype(f32) + b[at].astype(f32)
        send[i] = (a[away].astype(f32) + b[away].astype(f32)).astype(send.dtype)


def latent_sum_kernel(a, b, rope, out):
    lat = a.shape[2]
    out[:, :lat] = a[0] + b[0].astype(f32)
    out[:, lat:] = rope[...]


def fetch(value, offset, n):
    return lax.ppermute(value, "x", [(s, (s - offset) % n) for s in range(n)])


def trade(value, axes):
    return lax.all_to_all(value, axes, 0, 0, tiled=True)


def body(query, latent, dout, hidden):
    nw, nc, nz, ny, nx = (lax.axis_size(a) for a in ("w", "c", "z", "y", "x"))
    tok, heads, width = query.shape[1:]
    lat = dout.shape[3]
    rope = width - lat
    k_dev, model = hidden.shape[1:]
    rows = tok * heads
    n_rows, n_keys = nx * rows, nz * ny * k_dev
    pairs = n_rows * n_keys
    block = model // (nw * nc * nz * ny * nx)
    swap = [(0, 1), (1, 0)]
    pos = jnp.stack([lax.axis_index(a) for a in ("z", "y", "x")]).astype(jnp.int32)

    keys = trade(jnp.broadcast_to(latent, (nz * ny, k_dev, width)), ("z", "y"))
    (own,) = call(pack_kernel, [((rows, -(-(lat + width) // 128) * 128), bf16)], 2, moved=4 * rows * width)(
        dout.reshape(rows, lat), query.reshape(rows, width)
    )
    blocks = [own] + [fetch(own, k, nx) for k in range(1, nx)]

    wide = nw * nz * SLOT
    def halve(bit, a, b, token):
        n = nz >> (bit + 1)
        kept, sent, token = call(
            functools.partial(halve_kernel, bit), [((n, k_dev, lat), f32), ((n, k_dev, lat), bf16), TOKEN], 4,
            smem=(0,), unused=(3,), flops=8 * n * k_dev * lat, moved=12 * n * k_dev * lat,
        )(pos, a, b, token)
        return kept, lax.ppermute(sent, "z", [(i, i ^ (1 << bit)) for i in range(nz)]), token

    cols, token = call(
        functools.partial(columns_kernel, block, nz, ny * nx, nc), [((nc * ny * nx, k_dev, wide), bf16), TOKEN], 1,
        flops=2 * k_dev * model * 1024, moved=4 * k_dev * model, limit=20,
    )(hidden[0])
    e, dp, st = call(
        functools.partial(scores_kernel, lat, heads),
        [((n_keys, n_rows), f32)] * 2 + [((4 * nx, rows), f32)], 7, smem=(0,),
        unused=(2,),
        flops=2 * pairs * (width + lat), moved=8 * pairs, limit=20,
    )(pos, keys, token, *blocks)
    stats = trade(jnp.broadcast_to(st[None], (nx,) + st.shape), "x")
    rope_part, mine, other, dq_own, dq_keep, dq_send = call(
        functools.partial(dscores_kernel, lat),
        [((nz * ny, k_dev // 2, 2 * rope), bf16)] + [((nz, k_dev, lat), bf16)] * 2
        + [((rows, width), f32)] * 2 + [((rows, 2 * width), bf16)],
        10, smem=(0,), scratch=[pltpu.VMEM((n_keys, n_rows), bf16)] * 2,
        flops=2 * pairs * (2 * width + lat), moved=10 * pairs,
    )(pos, stats, st, e, dp, *blocks, keys)
    rope_part = trade(rope_part, ("z", "y"))
    dq_came = lax.ppermute(dq_send, "x", [(0, 1), (1, 0), (2, 3), (3, 2)])
    dq_own, dq_send, dq_token = call(
        query_half_kernel, [((rows, width), f32), ((rows, width), bf16), TOKEN], 3, moved=16 * rows * width
    )(dq_own, dq_keep, dq_came)
    dq_came = lax.ppermute(dq_send, "x", [(0, 3), (3, 0), (1, 2), (2, 1)])
    other = lax.ppermute(other, "y", swap)
    kept, came, token = halve(0, mine, other, token)
    rope_sum, terms = call(
        weight_kernel, [((k_dev, rope), f32), ((nc * ny * nx, rope, wide), bf16)], 4, unused=(2, 3),
        flops=2 * k_dev * nc * ny * nx * wide * rope, moved=4 * k_dev * model,
    )(rope_part, cols, token, dq_token)
    terms = trade(terms, ("c", "y", "x"))
    kept, came, token = halve(1, kept, came, token)
    terms, token = call(
        weight_half_kernel, [((nz, nw * SLOT // 2, 2 * rope), f32), TOKEN], 2, unused=(1,)
    )(terms, token)
    terms = trade(terms, "z")
    kept, came, token = halve(2, kept, came, token)
    (terms,) = call(weight_next_kernel, [((nw, SLOT // 2, 2 * rope), f32)], 1)(terms)
    terms = trade(terms, "w")
    dquery = (dq_own + dq_came.astype(f32)).astype(bf16)
    (dweight,) = call(weight_sum_kernel, [((block, rope), f32)], 1)(terms)
    (dlatent,) = call(latent_sum_kernel, [((k_dev, width), f32)], 3)(kept, came, rope_sum)

    return dquery.reshape(query.shape), dlatent[None], dweight


def solution(mesh):
    fine = Mesh(mesh.devices.reshape(4, 2, 8, 2, 4), ("w", "c", "z", "y", "x"))
    dp, sp = ("w", "c"), ("z", "y", "x")
    tokens = P(dp, sp, None, None)
    keys = P(dp, sp, None)
    return jax.shard_map(
        body,
        mesh=fine,
        in_specs=(tokens, keys, tokens, keys),
        out_specs=(tokens, keys, P(dp + sp, None)),
        check_vma=False,
    )
```

```python
import functools

import jax
import jax.numpy as jnp
from jax import lax
from jax.experimental import pallas as pl
from jax.experimental.pallas import tpu as pltpu
from jax.sharding import Mesh, PartitionSpec as P

softmax_scale = 0.07216878364870323
f32, bf16 = jnp.float32, jnp.bfloat16
TILE = 256
TOKEN = ((8, 128), jnp.float32)
SLOT = 16


def nt(a, b):
    return lax.dot_general(a, b, (((1,), (1,)), ((), ())), preferred_element_type=f32)


def nn(a, b):
    return lax.dot_general(a, b, (((1,), (0,)), ((), ())), preferred_element_type=f32)


def tn(a, b):
    return lax.dot_general(a, b, (((0,), (0,)), ((), ())), preferred_element_type=f32)


def call(kernel, outs, n_in, smem=(), unused=(), scratch=(), flops=0, moved=0, in_hbm=False, limit=20):
    vmem = pl.BlockSpec(memory_space=pltpu.VMEM)
    specs = [
        pl.BlockSpec(memory_space=pltpu.SMEM)
        if i in smem
        else (pl.BlockSpec(memory_space=pl.ANY) if i in unused else vmem)
        for i in range(n_in)
    ]
    return pl.pallas_call(
        kernel,
        out_shape=[pltpu.HBM(s, d) if in_hbm else jax.ShapeDtypeStruct(s, d) for s, d in outs],
        in_specs=specs,
        out_specs=[pl.BlockSpec(memory_space=pltpu.HBM) if in_hbm else vmem] * len(outs),
        scratch_shapes=scratch,
        compiler_params=pltpu.CompilerParams(vmem_limit_bytes=limit * 2**20),
        cost_estimate=pl.CostEstimate(flops=flops, bytes_accessed=moved, transcendentals=0),
    )


def pack_kernel(dout, query, out):
    lat = dout.shape[1]
    width = query.shape[1]
    out[:, :lat] = dout[...]
    out[:, lat : lat + width] = query[...]
    out[:, lat + width :] = jnp.zeros((out.shape[0], out.shape[1] - lat - width), out.dtype)


def columns_kernel(block, n_z, n_grp, n_core, hid, out, token):
    token[...] = jnp.zeros(token.shape, token.dtype)
    k_dev, model = hid.shape
    n_data = model // (n_z * n_grp * block)
    span = n_z * n_grp * block
    wide = n_z * SLOT
    c = lax.broadcasted_iota(jnp.int32, (span, n_grp * wide), 0)
    o = lax.broadcasted_iota(jnp.int32, (span, n_grp * wide), 1)
    g, zz, k = o // wide, (o % wide) // SLOT, o % SLOT
    pick = jnp.where((c == (zz * n_grp + g) * block + k) & (k < block), 1.0, 0.0).astype(bf16)
    stacked = jnp.concatenate([hid[:, d * span : (d + 1) * span] for d in range(n_data)])
    moved = nn(stacked, pick).astype(bf16)
    for d in range(n_data):
        first = d // n_core * wide
        for g in range(n_grp):
            out[d % n_core * n_grp + g, :, first : first + wide] = moved[
                d * k_dev : (d + 1) * k_dev, g * wide : (g + 1) * wide
            ]


def key_tile(keys, i, per):
    k = keys[i * per : (i + 1) * per]
    return k.reshape(k.shape[0] * k.shape[1], k.shape[2])


def scores_kernel(lat, heads, pos, keys, after, *refs):
    blocks, (e_ref, dp_ref, st_ref) = refs[:-3], refs[-3:]
    z, y, x = pos[0], pos[1], pos[2]
    grp, k_dev, width = keys.shape
    n_x = len(blocks)
    rows = refs[0].shape[0]
    n_keys = grp * k_dev
    tiles = n_keys // TILE
    per = TILE // k_dev
    tok = rows // heads
    first_query = grp * n_x * (k_dev - tok)
    for b, t in enumerate(blocks):
        q, o = t[:, lat : lat + width], t[:, :lat]
        cols = slice(b * rows, (b + 1) * rows)
        lane = lax.broadcasted_iota(jnp.int32, (k_dev, rows), 1)
        q_pos = ((z * 2 + y) * n_x + lax.rem(x + b, n_x)) * tok + lane // heads + first_query
        top = None
        for i in range(tiles):
            s = nt(key_tile(keys, i, per), q) * softmax_scale
            if i == tiles - 1:
                k_pos = ((grp - 1) * n_x + x) * k_dev + lax.broadcasted_iota(
                    jnp.int32, (k_dev, rows), 0
                )
                last = jnp.where(k_pos <= q_pos, s[TILE - k_dev :], -jnp.inf)
                s = jnp.concatenate([s[: TILE - k_dev], last])
            e_ref[i * TILE : (i + 1) * TILE, cols] = s
            m = jnp.max(s, axis=0, keepdims=True)
            top = m if top is None else jnp.maximum(top, m)
        total = jnp.zeros_like(top)
        delta = jnp.zeros_like(top)
        for i in range(tiles):
            part = slice(i * TILE, (i + 1) * TILE)
            dp = nt(key_tile(keys, i, per)[:, :lat], o)
            e = jnp.exp(e_ref[part, cols] - top)
            e_ref[part, cols] = e
            dp_ref[part, cols] = dp
            total += jnp.sum(e, axis=0, keepdims=True)
            delta += jnp.sum(e * dp, axis=0, keepdims=True)
        st_ref[4 * b : 4 * b + 4] = jnp.concatenate([top, total, delta, jnp.zeros_like(top)])


def dscores_kernel(lat, pos, stats, st, e_ref, dp_ref, *refs):
    n_x = stats.shape[0]
    blocks, outs, (sems, *held) = refs[:n_x], refs[n_x : n_x + 4], refs[n_x + 4 :]
    ds_ref, rope_ref, mine, other, p_ref = held
    copies = [pltpu.make_async_copy(held[i], outs[i], sems.at[i]) for i in range(4)]
    y, x = pos[1], pos[2]
    rows = refs[0].shape[0]
    tiles = e_ref.shape[0] // TILE
    grp, half_keys, _ = rope_ref.shape
    k_dev = 2 * half_keys
    for b in range(n_x):
        cols = slice(b * rows, (b + 1) * rows)
        theirs = []
        for s in range(n_x):
            at = lax.rem(x + b + n_x - s, n_x)
            v = stats[s, 0:4]
            for j in range(1, n_x):
                v = jnp.where(at == j, stats[s, 4 * j : 4 * j + 4], v)
            theirs.append(v)
        top = functools.reduce(jnp.maximum, [v[0:1] for v in theirs])
        w = [jnp.exp(v[0:1] - top) for v in theirs]
        total = sum(v[1:2] * u for v, u in zip(theirs, w))
        delta = sum(v[2:3] * u for v, u in zip(theirs, w)) / total
        f = jnp.exp(st[4 * b : 4 * b + 1] - top) / total
        for i in range(tiles):
            part = slice(i * TILE, (i + 1) * TILE)
            p = e_ref[part, cols] * f
            p_ref[part, cols] = p.astype(bf16)
            ds_ref[part, cols] = (p * (dp_ref[part, cols] - delta)).astype(bf16)
    copies[0].start()
    for i in range(tiles):
        part = slice(i * TILE, (i + 1) * TILE)
        r = None
        for b, t in enumerate(blocks):
            q = t[:, 2 * lat : 2 * lat + rope_ref.shape[2] // 2]
            v = nn(ds_ref[part, b * rows : (b + 1) * rows], q)
            r = v if r is None else r + v
        r = (r * softmax_scale).astype(bf16)
        for j in range(TILE // k_dev):
            k = r[j * k_dev : (j + 1) * k_dev]
            rope_ref[i * (TILE // k_dev) + j] = jnp.concatenate([k[:half_keys], k[half_keys:]], axis=1)
    copies[1].start()
    per = TILE // k_dev
    for i in range(tiles):
        part = slice(i * TILE, (i + 1) * TILE)
        v = None
        for b, t in enumerate(blocks):
            a = nn(ds_ref[part, b * rows : (b + 1) * rows], t[:, lat : 2 * lat])
            v = a if v is None else v + a
        v = v * softmax_scale
        for b, t in enumerate(blocks):
            v += nn(p_ref[part, b * rows : (b + 1) * rows], t[:, :lat])
        v = v.astype(bf16).reshape(per // 2, 2, k_dev, lat)
        first = i * per // 2
        for out, side in ((mine, y), (other, 1 - y)):
            out[first : first + per // 2] = jnp.where(side == 0, v[:, 0], v[:, 1])
    copies[2].start()
    copies[3].start()
    for copy in copies:
        copy.wait()


def query_kernel(ds_ref, keys, token, *outs):
    token[...] = jnp.zeros(token.shape, token.dtype)
    rows = outs[0].shape[0]
    per = TILE // keys.shape[1]
    for b, out in enumerate(outs):
        v = None
        for i in range(ds_ref.shape[0] // TILE):
            a = tn(
                ds_ref[i * TILE : (i + 1) * TILE, b * rows : (b + 1) * rows],
                key_tile(keys, i, per),
            )
            v = a if v is None else v + a
        out[...] = (v * softmax_scale).astype(out.dtype)


def weight_kernel(parts, cols, after, after2, rope_ref, out):
    v = jnp.sum(parts[...].astype(f32), axis=0)
    e = v.shape[1] // 2
    rope = jnp.concatenate([v[:, :e], v[:, e:]])
    rope_ref[...] = rope
    low = rope.astype(bf16)
    for i in range(cols.shape[0]):
        out[i] = tn(low, cols[i]).astype(bf16)


def weight_half_kernel(parts, after, out, token):
    token[...] = jnp.zeros(token.shape, token.dtype)
    v = jnp.sum(parts[...].astype(f32), axis=0)
    v = jnp.swapaxes(v, 0, 1)
    v = v.reshape(v.shape[0] // SLOT, SLOT, v.shape[1])
    out[...] = jnp.concatenate([v[:, : SLOT // 2], v[:, SLOT // 2 :]], axis=2)


def weight_sum_kernel(parts, out):
    v = jnp.sum(parts[...], axis=0)
    e = v.shape[1] // 2
    out[...] = jnp.concatenate([v[:, :e], v[:, e:]])[: out.shape[0]]


def halve_kernel(bit, pos, a, b, after, *refs):
    keep, send, token = refs
    token[...] = jnp.zeros(token.shape, token.dtype)
    mine = (pos[0] >> bit) & 1
    for i in range(keep.shape[0]):
        at, away = 2 * i + mine, 2 * i + 1 - mine
        keep[i] = a[at].astype(f32) + b[at].astype(f32)
        send[i] = (a[away].astype(f32) + b[away].astype(f32)).astype(send.dtype)


def latent_sum_kernel(a, b, rope, out):
    lat = a.shape[2]
    out[:, :lat] = a[0] + b[0].astype(f32)
    out[:, lat:] = rope[...]


def fetch(value, offset, n):
    return lax.ppermute(value, "x", [(s, (s - offset) % n) for s in range(n)])


def trade(value, axes):
    return lax.all_to_all(value, axes, 0, 0, tiled=True)


def body(query, latent, dout, hidden):
    nw, nc, nz, ny, nx = (lax.axis_size(a) for a in ("w", "c", "z", "y", "x"))
    tok, heads, width = query.shape[1:]
    lat = dout.shape[3]
    rope = width - lat
    k_dev, model = hidden.shape[1:]
    rows = tok * heads
    n_rows, n_keys = nx * rows, nz * ny * k_dev
    pairs = n_rows * n_keys
    block = model // (nw * nc * nz * ny * nx)
    swap = [(0, 1), (1, 0)]
    pos = jnp.stack([lax.axis_index(a) for a in ("z", "y", "x")]).astype(jnp.int32)

    keys = trade(jnp.broadcast_to(latent, (nz * ny, k_dev, width)), ("z", "y"))
    (own,) = call(pack_kernel, [((rows, -(-(lat + width) // 128) * 128), bf16)], 2, moved=4 * rows * width)(
        dout.reshape(rows, lat), query.reshape(rows, width)
    )
    blocks = [own] + [fetch(own, k, nx) for k in range(1, nx)]

    wide = nw * nz * SLOT
    cols, token = call(
        functools.partial(columns_kernel, block, nz, ny * nx, nc), [((nc * ny * nx, k_dev, wide), bf16), TOKEN], 1,
        flops=2 * k_dev * model * 1024, moved=4 * k_dev * model, limit=20,
    )(hidden[0])
    e, dp, st = call(
        functools.partial(scores_kernel, lat, heads),
        [((n_keys, n_rows), f32)] * 2 + [((4 * nx, rows), f32)], 7, smem=(0,),
        unused=(2,),
        flops=2 * pairs * (width + lat), moved=8 * pairs, limit=20,
    )(pos, keys, token, *blocks)
    stats = trade(jnp.broadcast_to(st[None], (nx,) + st.shape), "x")
    ds, rope_part, mine, other = call(
        functools.partial(dscores_kernel, lat),
        [((n_keys, n_rows), bf16), ((nz * ny, k_dev // 2, 2 * rope), bf16)] + [((nz, k_dev, lat), bf16)] * 2,
        9, smem=(0,), in_hbm=True,
        scratch=[
            pltpu.SemaphoreType.DMA((4,)),
            pltpu.VMEM((n_keys, n_rows), bf16),
            pltpu.VMEM((nz * ny, k_dev // 2, 2 * rope), bf16),
            pltpu.VMEM((nz, k_dev, lat), bf16),
            pltpu.VMEM((nz, k_dev, lat), bf16),
            pltpu.VMEM((n_keys, n_rows), bf16),
        ],
        flops=2 * pairs * (rope + 2 * lat), moved=12 * pairs,
    )(pos, stats, st, e, dp, *blocks)
    rope_part = trade(rope_part, ("z", "y"))
    other = lax.ppermute(other, "y", swap)
    dq_token, *dq = call(
        query_kernel, [TOKEN, ((rows, width), f32)] + [((rows, width), bf16)] * (nx - 1), 2,
        flops=2 * pairs * width, moved=4 * pairs,
    )(ds, keys)
    rope_sum, terms = call(
        weight_kernel, [((k_dev, rope), f32), ((nc * ny * nx, rope, wide), bf16)], 4, unused=(2, 3),
        flops=2 * k_dev * nc * ny * nx * wide * rope, moved=4 * k_dev * model, limit=20,
    )(rope_part, cols, other, dq_token)
    terms = trade(terms, ("c", "y", "x"))
    dq = [dq[0]] + [fetch(dq[k], nx - k, nx) for k in range(1, nx)]
    kept, came = mine, other
    for bit in range(3):
        if bit == 2:
            terms, token = call(
                weight_half_kernel, [((nw * nz, SLOT // 2, 2 * rope), f32), TOKEN], 2, unused=(1,)
            )(terms, token)
            terms = trade(terms, ("w", "z"))
        n = nz >> (bit + 1)
        kept, sent, token = call(
            functools.partial(halve_kernel, bit), [((n, k_dev, lat), f32), ((n, k_dev, lat), bf16), TOKEN], 4,
            smem=(0,), unused=(3,), flops=8 * n * k_dev * lat, moved=12 * n * k_dev * lat, limit=20,
        )(pos, kept, came, token)
        came = lax.ppermute(sent, "z", [(i, i ^ (1 << bit)) for i in range(nz)])
    (dweight,) = call(weight_sum_kernel, [((block, rope), f32)], 1)(terms)
    (dlatent,) = call(latent_sum_kernel, [((k_dev, width), f32)], 3)(kept, came, rope_sum)

    total = dq[0]
    for part in dq[1:]:
        total = total + part.astype(f32)
    return total.astype(bf16).reshape(query.shape), dlatent[None], dweight


def solution(mesh):
    fine = Mesh(mesh.devices.reshape(4, 2, 8, 2, 4), ("w", "c", "z", "y", "x"))
    dp, sp = ("w", "c"), ("z", "y", "x")
    tokens = P(dp, sp, None, None)
    keys = P(dp, sp, None)
    return jax.shard_map(
        body,
        mesh=fine,
        in_specs=(tokens, keys, tokens, keys),
        out_specs=(tokens, keys, P(dp + sp, None)),
        check_vma=False,
    )
```

```python
import functools

import jax
import jax.numpy as jnp
from jax import lax
from jax.experimental import pallas as pl
from jax.experimental.pallas import tpu as pltpu
from jax.sharding import Mesh, PartitionSpec as P

softmax_scale = 0.07216878364870323
f32, bf16 = jnp.float32, jnp.bfloat16
TILE = 256
TOKEN = ((8, 128), jnp.float32)
SLOT = 16


def nt(a, b):
    return lax.dot_general(a, b, (((1,), (1,)), ((), ())), preferred_element_type=f32)


def nn(a, b):
    return lax.dot_general(a, b, (((1,), (0,)), ((), ())), preferred_element_type=f32)


def tn(a, b):
    return lax.dot_general(a, b, (((0,), (0,)), ((), ())), preferred_element_type=f32)


def call(kernel, outs, n_in, smem=(), unused=(), scratch=(), flops=0, moved=0, in_hbm=False, limit=20):
    vmem = pl.BlockSpec(memory_space=pltpu.VMEM)
    specs = [
        pl.BlockSpec(memory_space=pltpu.SMEM)
        if i in smem
        else (pl.BlockSpec(memory_space=pl.ANY) if i in unused else vmem)
        for i in range(n_in)
    ]
    return pl.pallas_call(
        kernel,
        out_shape=[pltpu.HBM(s, d) if in_hbm else jax.ShapeDtypeStruct(s, d) for s, d in outs],
        in_specs=specs,
        out_specs=[pl.BlockSpec(memory_space=pltpu.HBM) if in_hbm else vmem] * len(outs),
        scratch_shapes=scratch,
        compiler_params=pltpu.CompilerParams(vmem_limit_bytes=limit * 2**20),
        cost_estimate=pl.CostEstimate(flops=flops, bytes_accessed=moved, transcendentals=0),
    )


def pack_kernel(dout, query, out):
    lat = dout.shape[1]
    width = query.shape[1]
    out[:, :lat] = dout[...]
    out[:, lat : lat + width] = query[...]
    out[:, lat + width :] = jnp.zeros((out.shape[0], out.shape[1] - lat - width), out.dtype)


def columns_kernel(block, n_z, n_grp, n_core, hid, out, token):
    token[...] = jnp.zeros(token.shape, token.dtype)
    k_dev, model = hid.shape
    n_data = model // (n_z * n_grp * block)
    span = n_z * n_grp * block
    wide = n_z * SLOT
    c = lax.broadcasted_iota(jnp.int32, (span, n_grp * wide), 0)
    o = lax.broadcasted_iota(jnp.int32, (span, n_grp * wide), 1)
    g, zz, k = o // wide, (o % wide) // SLOT, o % SLOT
    pick = jnp.where((c == (zz * n_grp + g) * block + k) & (k < block), 1.0, 0.0).astype(bf16)
    stacked = jnp.concatenate([hid[:, d * span : (d + 1) * span] for d in range(n_data)])
    moved = nn(stacked, pick).astype(bf16)
    for d in range(n_data):
        first = d // n_core * wide
        for g in range(n_grp):
            out[d % n_core * n_grp + g, :, first : first + wide] = moved[
                d * k_dev : (d + 1) * k_dev, g * wide : (g + 1) * wide
            ]


def key_tile(keys, i, per):
    k = keys[i * per : (i + 1) * per]
    return k.reshape(k.shape[0] * k.shape[1], k.shape[2])


def scores_kernel(lat, heads, pos, keys, after, *refs):
    blocks, (e_ref, dp_ref, st_ref) = refs[:-3], refs[-3:]
    z, y, x = pos[0], pos[1], pos[2]
    grp, k_dev, width = keys.shape
    n_x = len(blocks)
    rows = refs[0].shape[0]
    n_keys = grp * k_dev
    tiles = n_keys // TILE
    per = TILE // k_dev
    tok = rows // heads
    first_query = grp * n_x * (k_dev - tok)
    for b, t in enumerate(blocks):
        q, o = t[:, lat : lat + width], t[:, :lat]
        cols = slice(b * rows, (b + 1) * rows)
        lane = lax.broadcasted_iota(jnp.int32, (k_dev, rows), 1)
        q_pos = ((z * 2 + y) * n_x + lax.rem(x + b, n_x)) * tok + lane // heads + first_query
        top = None
        for i in range(tiles):
            s = nt(key_tile(keys, i, per), q) * softmax_scale
            if i == tiles - 1:
                k_pos = ((grp - 1) * n_x + x) * k_dev + lax.broadcasted_iota(
                    jnp.int32, (k_dev, rows), 0
                )
                last = jnp.where(k_pos <= q_pos, s[TILE - k_dev :], -jnp.inf)
                s = jnp.concatenate([s[: TILE - k_dev], last])
            e_ref[i * TILE : (i + 1) * TILE, cols] = s
            m = jnp.max(s, axis=0, keepdims=True)
            top = m if top is None else jnp.maximum(top, m)
        total = jnp.zeros_like(top)
        delta = jnp.zeros_like(top)
        for i in range(tiles):
            part = slice(i * TILE, (i + 1) * TILE)
            dp = nt(key_tile(keys, i, per)[:, :lat], o)
            e = jnp.exp(e_ref[part, cols] - top)
            e_ref[part, cols] = e
            dp_ref[part, cols] = dp
            total += jnp.sum(e, axis=0, keepdims=True)
            delta += jnp.sum(e * dp, axis=0, keepdims=True)
        st_ref[4 * b : 4 * b + 4] = jnp.concatenate([top, total, delta, jnp.zeros_like(top)])


def dscores_kernel(lat, pos, stats, st, e_ref, dp_ref, *refs):
    n_x = stats.shape[0]
    blocks, outs, (sems, *held) = refs[:n_x], refs[n_x : n_x + 4], refs[n_x + 4 :]
    ds_ref, rope_ref, mine, other, p_ref = held
    copies = [pltpu.make_async_copy(held[i], outs[i], sems.at[i]) for i in range(4)]
    y, x = pos[1], pos[2]
    rows = refs[0].shape[0]
    tiles = e_ref.shape[0] // TILE
    grp, half_keys, _ = rope_ref.shape
    k_dev = 2 * half_keys
    for b in range(n_x):
        cols = slice(b * rows, (b + 1) * rows)
        theirs = []
        for s in range(n_x):
            at = lax.rem(x + b + n_x - s, n_x)
            v = stats[s, 0:4]
            for j in range(1, n_x):
                v = jnp.where(at == j, stats[s, 4 * j : 4 * j + 4], v)
            theirs.append(v)
        top = functools.reduce(jnp.maximum, [v[0:1] for v in theirs])
        w = [jnp.exp(v[0:1] - top) for v in theirs]
        total = sum(v[1:2] * u for v, u in zip(theirs, w))
        delta = sum(v[2:3] * u for v, u in zip(theirs, w)) / total
        f = jnp.exp(st[4 * b : 4 * b + 1] - top) / total
        for i in range(tiles):
            part = slice(i * TILE, (i + 1) * TILE)
            p = e_ref[part, cols] * f
            p_ref[part, cols] = p.astype(bf16)
            ds_ref[part, cols] = (p * (dp_ref[part, cols] - delta)).astype(bf16)
    copies[0].start()
    for i in range(tiles):
        part = slice(i * TILE, (i + 1) * TILE)
        r = None
        for b, t in enumerate(blocks):
            q = t[:, 2 * lat : 2 * lat + rope_ref.shape[2] // 2]
            v = nn(ds_ref[part, b * rows : (b + 1) * rows], q)
            r = v if r is None else r + v
        r = (r * softmax_scale).astype(bf16)
        for j in range(TILE // k_dev):
            k = r[j * k_dev : (j + 1) * k_dev]
            rope_ref[i * (TILE // k_dev) + j] = jnp.concatenate([k[:half_keys], k[half_keys:]], axis=1)
    copies[1].start()
    per = TILE // k_dev
    for i in range(tiles):
        part = slice(i * TILE, (i + 1) * TILE)
        v = None
        for b, t in enumerate(blocks):
            a = nn(ds_ref[part, b * rows : (b + 1) * rows], t[:, lat : 2 * lat])
            v = a if v is None else v + a
        v = v * softmax_scale
        for b, t in enumerate(blocks):
            v += nn(p_ref[part, b * rows : (b + 1) * rows], t[:, :lat])
        v = v.astype(bf16).reshape(per // 2, 2, k_dev, lat)
        first = i * per // 2
        for out, side in ((mine, y), (other, 1 - y)):
            out[first : first + per // 2] = jnp.where(side == 0, v[:, 0], v[:, 1])
    copies[2].start()
    copies[3].start()
    for copy in copies:
        copy.wait()


def query_kernel(ds_ref, keys, token, *outs):
    token[...] = jnp.zeros(token.shape, token.dtype)
    rows = outs[0].shape[0]
    per = TILE // keys.shape[1]
    for b, out in enumerate(outs):
        v = None
        for i in range(ds_ref.shape[0] // TILE):
            a = tn(
                ds_ref[i * TILE : (i + 1) * TILE, b * rows : (b + 1) * rows],
                key_tile(keys, i, per),
            )
            v = a if v is None else v + a
        out[...] = (v * softmax_scale).astype(out.dtype)


def query_hop_kernel(keep, came, send, token):
    token[...] = jnp.zeros(token.shape, token.dtype)
    send[...] = (keep[...].astype(f32) + came[...].astype(f32)).astype(send.dtype)


def weight_kernel(parts, cols, after, after2, rope_ref, out):
    v = jnp.sum(parts[...].astype(f32), axis=0)
    e = v.shape[1] // 2
    rope = jnp.concatenate([v[:, :e], v[:, e:]])
    rope_ref[...] = rope
    low = rope.astype(bf16)
    for i in range(cols.shape[0]):
        out[i] = tn(low, cols[i]).astype(bf16)


def weight_half_kernel(parts, after, after2, out, token):
    token[...] = jnp.zeros(token.shape, token.dtype)
    v = jnp.sum(parts[...].astype(f32), axis=0)
    v = jnp.swapaxes(v, 0, 1)
    v = v.reshape(v.shape[0] // SLOT, SLOT, v.shape[1])
    out[...] = jnp.concatenate([v[:, : SLOT // 2], v[:, SLOT // 2 :]], axis=2)


def weight_sum_kernel(parts, out):
    v = jnp.sum(parts[...], axis=0)
    e = v.shape[1] // 2
    out[...] = jnp.concatenate([v[:, :e], v[:, e:]])[: out.shape[0]]


def halve_kernel(bit, pos, a, b, after, *refs):
    keep, send, token = refs
    token[...] = jnp.zeros(token.shape, token.dtype)
    mine = (pos[0] >> bit) & 1
    for i in range(keep.shape[0]):
        at, away = 2 * i + mine, 2 * i + 1 - mine
        keep[i] = a[at].astype(f32) + b[at].astype(f32)
        send[i] = (a[away].astype(f32) + b[away].astype(f32)).astype(send.dtype)


def latent_sum_kernel(a, b, rope, out):
    lat = a.shape[2]
    out[:, :lat] = a[0] + b[0].astype(f32)
    out[:, lat:] = rope[...]


def fetch(value, offset, n):
    return lax.ppermute(value, "x", [(s, (s - offset) % n) for s in range(n)])


def trade(value, axes):
    return lax.all_to_all(value, axes, 0, 0, tiled=True)


def body(query, latent, dout, hidden):
    nw, nc, nz, ny, nx = (lax.axis_size(a) for a in ("w", "c", "z", "y", "x"))
    tok, heads, width = query.shape[1:]
    lat = dout.shape[3]
    rope = width - lat
    k_dev, model = hidden.shape[1:]
    rows = tok * heads
    n_rows, n_keys = nx * rows, nz * ny * k_dev
    pairs = n_rows * n_keys
    block = model // (nw * nc * nz * ny * nx)
    swap = [(0, 1), (1, 0)]
    pos = jnp.stack([lax.axis_index(a) for a in ("z", "y", "x")]).astype(jnp.int32)

    keys = trade(jnp.broadcast_to(latent, (nz * ny, k_dev, width)), ("z", "y"))
    (own,) = call(pack_kernel, [((rows, -(-(lat + width) // 128) * 128), bf16)], 2, moved=4 * rows * width)(
        dout.reshape(rows, lat), query.reshape(rows, width)
    )
    blocks = [own] + [fetch(own, k, nx) for k in range(1, nx)]

    wide = nw * nz * SLOT
    cols, token = call(
        functools.partial(columns_kernel, block, nz, ny * nx, nc), [((nc * ny * nx, k_dev, wide), bf16), TOKEN], 1,
        flops=2 * k_dev * model * 1024, moved=4 * k_dev * model, limit=20,
    )(hidden[0])
    e, dp, st = call(
        functools.partial(scores_kernel, lat, heads),
        [((n_keys, n_rows), f32)] * 2 + [((4 * nx, rows), f32)], 7, smem=(0,),
        unused=(2,),
        flops=2 * pairs * (width + lat), moved=8 * pairs, limit=20,
    )(pos, keys, token, *blocks)
    stats = trade(jnp.broadcast_to(st[None], (nx,) + st.shape), "x")
    ds, rope_part, mine, other = call(
        functools.partial(dscores_kernel, lat),
        [((n_keys, n_rows), bf16), ((nz * ny, k_dev // 2, 2 * rope), bf16)] + [((nz, k_dev, lat), bf16)] * 2,
        9, smem=(0,), in_hbm=True,
        scratch=[
            pltpu.SemaphoreType.DMA((4,)),
            pltpu.VMEM((n_keys, n_rows), bf16),
            pltpu.VMEM((nz * ny, k_dev // 2, 2 * rope), bf16),
            pltpu.VMEM((nz, k_dev, lat), bf16),
            pltpu.VMEM((nz, k_dev, lat), bf16),
            pltpu.VMEM((n_keys, n_rows), bf16),
        ],
        flops=2 * pairs * (rope + 2 * lat), moved=12 * pairs,
    )(pos, stats, st, e, dp, *blocks)
    rope_part = trade(rope_part, ("z", "y"))
    other = lax.ppermute(other, "y", swap)
    dq_token, *dq = call(
        query_kernel, [TOKEN, ((rows, width), f32)] + [((rows, width), bf16)] * (nx - 1), 2,
        flops=2 * pairs * width, moved=4 * pairs,
    )(ds, keys)
    rope_sum, terms = call(
        weight_kernel, [((k_dev, rope), f32), ((nc * ny * nx, rope, wide), bf16)], 4, unused=(2, 3),
        flops=2 * k_dev * nc * ny * nx * wide * rope, moved=4 * k_dev * model, limit=20,
    )(rope_part, cols, other, dq_token)
    terms = trade(terms, ("c", "y", "x"))
    came = fetch(dq[2], nx - 1, nx)
    dq_send, dq_token = call(query_hop_kernel, [((rows, width), bf16), TOKEN], 2)(dq[1], came)
    dq = [dq[0], fetch(dq_send, nx - 1, nx), fetch(dq[3], 1, nx)]
    kept, came = mine, other
    for bit in range(3):
        if bit == 2:
            terms, token = call(
                weight_half_kernel, [((nw * nz, SLOT // 2, 2 * rope), f32), TOKEN], 3, unused=(1, 2)
            )(terms, token, dq_token)
            terms = trade(terms, ("w", "z"))
        n = nz >> (bit + 1)
        kept, sent, token = call(
            functools.partial(halve_kernel, bit), [((n, k_dev, lat), f32), ((n, k_dev, lat), bf16), TOKEN], 4,
            smem=(0,), unused=(3,), flops=8 * n * k_dev * lat, moved=12 * n * k_dev * lat, limit=20,
        )(pos, kept, came, token)
        came = lax.ppermute(sent, "z", [(i, i ^ (1 << bit)) for i in range(nz)])
    (dweight,) = call(weight_sum_kernel, [((block, rope), f32)], 1)(terms)
    (dlatent,) = call(latent_sum_kernel, [((k_dev, width), f32)], 3)(kept, came, rope_sum)

    total = dq[0]
    for part in dq[1:]:
        total = total + part.astype(f32)
    return total.astype(bf16).reshape(query.shape), dlatent[None], dweight


def solution(mesh):
    fine = Mesh(mesh.devices.reshape(4, 2, 8, 2, 4), ("w", "c", "z", "y", "x"))
    dp, sp = ("w", "c"), ("z", "y", "x")
    tokens = P(dp, sp, None, None)
    keys = P(dp, sp, None)
    return jax.shard_map(
        body,
        mesh=fine,
        in_specs=(tokens, keys, tokens, keys),
        out_specs=(tokens, keys, P(dp + sp, None)),
        check_vma=False,
    )
```

```python
import functools

import jax
import jax.numpy as jnp
from jax import lax
from jax.experimental import pallas as pl
from jax.experimental.pallas import tpu as pltpu
from jax.sharding import Mesh, PartitionSpec as P

softmax_scale = 0.07216878364870323
f32, bf16 = jnp.float32, jnp.bfloat16
TILE = 256
Z = ("zh", "zl")
TOKEN = ((8, 128), jnp.float32)
SLOT = 16


def nt(a, b):
    return lax.dot_general(a, b, (((1,), (1,)), ((), ())), preferred_element_type=f32)


def nn(a, b):
    return lax.dot_general(a, b, (((1,), (0,)), ((), ())), preferred_element_type=f32)


def tn(a, b):
    return lax.dot_general(a, b, (((0,), (0,)), ((), ())), preferred_element_type=f32)


def call(kernel, outs, n_in, smem=(), unused=(), scratch=(), flops=0, moved=0, in_hbm=False, limit=20):
    vmem = pl.BlockSpec(memory_space=pltpu.VMEM)
    specs = [
        pl.BlockSpec(memory_space=pltpu.SMEM)
        if i in smem
        else (pl.BlockSpec(memory_space=pl.ANY) if i in unused else vmem)
        for i in range(n_in)
    ]
    return pl.pallas_call(
        kernel,
        out_shape=[pltpu.HBM(s, d) if in_hbm else jax.ShapeDtypeStruct(s, d) for s, d in outs],
        in_specs=specs,
        out_specs=[pl.BlockSpec(memory_space=pltpu.HBM) if in_hbm else vmem] * len(outs),
        scratch_shapes=scratch,
        compiler_params=pltpu.CompilerParams(vmem_limit_bytes=limit * 2**20),
        cost_estimate=pl.CostEstimate(flops=flops, bytes_accessed=moved, transcendentals=0),
    )


def pack_kernel(dout, query, out):
    lat = dout.shape[1]
    width = query.shape[1]
    out[:, :lat] = dout[...]
    out[:, lat : lat + width] = query[...]
    out[:, lat + width :] = jnp.zeros((out.shape[0], out.shape[1] - lat - width), out.dtype)


def columns_kernel(block, n_z, n_low, n_grp, n_core, hid, out, token):
    token[...] = jnp.zeros(token.shape, token.dtype)
    k_dev, model = hid.shape
    n_data = model // (n_z * n_grp * block)
    span = n_z * n_grp * block
    wide = n_z * SLOT
    c = lax.broadcasted_iota(jnp.int32, (span, n_grp * wide), 0)
    o = lax.broadcasted_iota(jnp.int32, (span, n_grp * wide), 1)
    g, k = o // wide, o % SLOT
    n_high = n_z // n_low
    zz = (o % wide) // SLOT
    zz = zz % n_high * n_low + zz // n_high
    pick = jnp.where((c == (zz * n_grp + g) * block + k) & (k < block), 1.0, 0.0).astype(bf16)
    stacked = jnp.concatenate([hid[:, d * span : (d + 1) * span] for d in range(n_data)])
    moved = nn(stacked, pick).astype(bf16)
    for d in range(n_data):
        part = wide // n_low
        first = d // n_core * part
        for low in range(n_low):
            for g in range(n_grp):
                at = g * wide + low * part
                out[(d % n_core * n_low + low) * n_grp + g, :, first : first + part] = moved[
                    d * k_dev : (d + 1) * k_dev, at : at + part
                ]


def key_tile(keys, i, per):
    k = keys[i * per : (i + 1) * per]
    return k.reshape(k.shape[0] * k.shape[1], k.shape[2])


def scores_kernel(lat, heads, pos, keys, after, *refs):
    blocks, (e_ref, dp_ref, st_ref) = refs[:-3], refs[-3:]
    z, y, x = pos[0], pos[1], pos[2]
    grp, k_dev, width = keys.shape
    n_x = len(blocks)
    rows = refs[0].shape[0]
    n_keys = grp * k_dev
    tiles = n_keys // TILE
    per = TILE // k_dev
    tok = rows // heads
    first_query = grp * n_x * (k_dev - tok)
    for b, t in enumerate(blocks):
        q, o = t[:, lat : lat + width], t[:, :lat]
        cols = slice(b * rows, (b + 1) * rows)
        lane = lax.broadcasted_iota(jnp.int32, (k_dev, rows), 1)
        q_pos = ((z * 2 + y) * n_x + lax.rem(x + b, n_x)) * tok + lane // heads + first_query
        top = None
        for i in range(tiles):
            s = nt(key_tile(keys, i, per), q) * softmax_scale
            if i == tiles - 1:
                k_pos = ((grp - 1) * n_x + x) * k_dev + lax.broadcasted_iota(
                    jnp.int32, (k_dev, rows), 0
                )
                last = jnp.where(k_pos <= q_pos, s[TILE - k_dev :], -jnp.inf)
                s = jnp.concatenate([s[: TILE - k_dev], last])
            e_ref[i * TILE : (i + 1) * TILE, cols] = s
            m = jnp.max(s, axis=0, keepdims=True)
            top = m if top is None else jnp.maximum(top, m)
        total = jnp.zeros_like(top)
        delta = jnp.zeros_like(top)
        for i in range(tiles):
            part = slice(i * TILE, (i + 1) * TILE)
            dp = nt(key_tile(keys, i, per)[:, :lat], o)
            e = jnp.exp(e_ref[part, cols] - top)
            e_ref[part, cols] = e
            dp_ref[part, cols] = dp
            total += jnp.sum(e, axis=0, keepdims=True)
            delta += jnp.sum(e * dp, axis=0, keepdims=True)
        st_ref[4 * b : 4 * b + 4] = jnp.concatenate([top, total, delta, jnp.zeros_like(top)])


def dscores_kernel(lat, pos, stats, st, e_ref, dp_ref, *refs):
    n_x = stats.shape[0]
    blocks, outs, (sems, *held) = refs[:n_x], refs[n_x : n_x + 4], refs[n_x + 4 :]
    ds_ref, rope_ref, mine, other, p_ref = held
    copies = [pltpu.make_async_copy(held[i], outs[i], sems.at[i]) for i in range(4)]
    y, x = pos[1], pos[2]
    rows = refs[0].shape[0]
    tiles = e_ref.shape[0] // TILE
    grp, half_keys, _ = rope_ref.shape
    k_dev = 2 * half_keys
    for b in range(n_x):
        cols = slice(b * rows, (b + 1) * rows)
        theirs = []
        for s in range(n_x):
            at = lax.rem(x + b + n_x - s, n_x)
            v = stats[s, 0:4]
            for j in range(1, n_x):
                v = jnp.where(at == j, stats[s, 4 * j : 4 * j + 4], v)
            theirs.append(v)
        top = functools.reduce(jnp.maximum, [v[0:1] for v in theirs])
        w = [jnp.exp(v[0:1] - top) for v in theirs]
        total = sum(v[1:2] * u for v, u in zip(theirs, w))
        delta = sum(v[2:3] * u for v, u in zip(theirs, w)) / total
        f = jnp.exp(st[4 * b : 4 * b + 1] - top) / total
        for i in range(tiles):
            part = slice(i * TILE, (i + 1) * TILE)
            p = e_ref[part, cols] * f
            p_ref[part, cols] = p.astype(bf16)
            ds_ref[part, cols] = (p * (dp_ref[part, cols] - delta)).astype(bf16)
    copies[0].start()
    for i in range(tiles):
        part = slice(i * TILE, (i + 1) * TILE)
        r = None
        for b, t in enumerate(blocks):
            q = t[:, 2 * lat : 2 * lat + rope_ref.shape[2] // 2]
            v = nn(ds_ref[part, b * rows : (b + 1) * rows], q)
            r = v if r is None else r + v
        r = (r * softmax_scale).astype(bf16)
        for j in range(TILE // k_dev):
            k = r[j * k_dev : (j + 1) * k_dev]
            rope_ref[i * (TILE // k_dev) + j] = jnp.concatenate([k[:half_keys], k[half_keys:]], axis=1)
    copies[1].start()
    per = TILE // k_dev
    for i in range(tiles):
        part = slice(i * TILE, (i + 1) * TILE)
        v = None
        for b, t in enumerate(blocks):
            a = nn(ds_ref[part, b * rows : (b + 1) * rows], t[:, lat : 2 * lat])
            v = a if v is None else v + a
        v = v * softmax_scale
        for b, t in enumerate(blocks):
            v += nn(p_ref[part, b * rows : (b + 1) * rows], t[:, :lat])
        v = v.astype(bf16).reshape(per // 2, 2, k_dev, lat)
        first = i * per // 2
        for out, side in ((mine, y), (other, 1 - y)):
            out[first : first + per // 2] = jnp.where(side == 0, v[:, 0], v[:, 1])
    copies[2].start()
    copies[3].start()
    for copy in copies:
        copy.wait()


def query_kernel(ds_ref, keys, token, *outs):
    token[...] = jnp.zeros(token.shape, token.dtype)
    rows = outs[0].shape[0]
    per = TILE // keys.shape[1]
    for b, out in enumerate(outs):
        v = None
        for i in range(ds_ref.shape[0] // TILE):
            a = tn(
                ds_ref[i * TILE : (i + 1) * TILE, b * rows : (b + 1) * rows],
                key_tile(keys, i, per),
            )
            v = a if v is None else v + a
        out[...] = (v * softmax_scale).astype(out.dtype)


def weight_kernel(parts, cols, after, after2, rope_ref, out):
    v = jnp.sum(parts[...].astype(f32), axis=0)
    e = v.shape[1] // 2
    rope = jnp.concatenate([v[:, :e], v[:, e:]])
    rope_ref[...] = rope
    low = rope.astype(bf16)
    for i in range(cols.shape[0]):
        out[i] = tn(low, cols[i]).astype(bf16)


def weight_half_kernel(parts, after, out, token):
    token[...] = jnp.zeros(token.shape, token.dtype)
    v = jnp.sum(parts[...].astype(f32), axis=0)
    v = jnp.swapaxes(v, 0, 1)
    v = v.reshape(v.shape[0] // SLOT, SLOT, v.shape[1])
    out[...] = jnp.concatenate([v[:, : SLOT // 2], v[:, SLOT // 2 :]], axis=2)


def weight_sum_kernel(parts, out):
    v = jnp.sum(parts[...], axis=0)
    e = v.shape[1] // 2
    out[...] = jnp.concatenate([v[:, :e], v[:, e:]])[: out.shape[0]]


def halve_kernel(bit, pos, a, b, after, *refs):
    keep, send, token = refs
    token[...] = jnp.zeros(token.shape, token.dtype)
    mine = (pos[0] >> bit) & 1
    for i in range(keep.shape[0]):
        at, away = 2 * i + mine, 2 * i + 1 - mine
        keep[i] = a[at].astype(f32) + b[at].astype(f32)
        send[i] = (a[away].astype(f32) + b[away].astype(f32)).astype(send.dtype)


def latent_sum_kernel(a, b, rope, out):
    lat = a.shape[2]
    out[:, :lat] = a[0] + b[0].astype(f32)
    out[:, lat:] = rope[...]


def fetch(value, offset, n):
    return lax.ppermute(value, "x", [(s, (s - offset) % n) for s in range(n)])


def trade(value, axes):
    return lax.all_to_all(value, axes, 0, 0, tiled=True)


def body(query, latent, dout, hidden):
    nw, nc, nh, nl, ny, nx = (lax.axis_size(a) for a in ("w", "c", "zh", "zl", "y", "x"))
    nz = nh * nl
    tok, heads, width = query.shape[1:]
    lat = dout.shape[3]
    rope = width - lat
    k_dev, model = hidden.shape[1:]
    rows = tok * heads
    n_rows, n_keys = nx * rows, nz * ny * k_dev
    pairs = n_rows * n_keys
    block = model // (nw * nc * nz * ny * nx)
    swap = [(0, 1), (1, 0)]
    pos = jnp.stack([lax.axis_index(a) for a in (Z, "y", "x")]).astype(jnp.int32)

    keys = trade(jnp.broadcast_to(latent, (nz * ny, k_dev, width)), Z + ("y",))
    (own,) = call(pack_kernel, [((rows, -(-(lat + width) // 128) * 128), bf16)], 2, moved=4 * rows * width)(
        dout.reshape(rows, lat), query.reshape(rows, width)
    )
    blocks = [own] + [fetch(own, k, nx) for k in range(1, nx)]

    wide = nw * nh * SLOT
    cols, token = call(
        functools.partial(columns_kernel, block, nz, nl, ny * nx, nc),
        [((nc * nl * ny * nx, k_dev, wide), bf16), TOKEN], 1,
        flops=2 * k_dev * model * 1024, moved=4 * k_dev * model, limit=20,
    )(hidden[0])
    e, dp, st = call(
        functools.partial(scores_kernel, lat, heads),
        [((n_keys, n_rows), f32)] * 2 + [((4 * nx, rows), f32)], 7, smem=(0,),
        unused=(2,),
        flops=2 * pairs * (width + lat), moved=8 * pairs, limit=20,
    )(pos, keys, token, *blocks)
    stats = trade(jnp.broadcast_to(st[None], (nx,) + st.shape), "x")
    ds, rope_part, mine, other = call(
        functools.partial(dscores_kernel, lat),
        [((n_keys, n_rows), bf16), ((nz * ny, k_dev // 2, 2 * rope), bf16)] + [((nz, k_dev, lat), bf16)] * 2,
        9, smem=(0,), in_hbm=True,
        scratch=[
            pltpu.SemaphoreType.DMA((4,)),
            pltpu.VMEM((n_keys, n_rows), bf16),
            pltpu.VMEM((nz * ny, k_dev // 2, 2 * rope), bf16),
            pltpu.VMEM((nz, k_dev, lat), bf16),
            pltpu.VMEM((nz, k_dev, lat), bf16),
            pltpu.VMEM((n_keys, n_rows), bf16),
        ],
        flops=2 * pairs * (rope + 2 * lat), moved=12 * pairs,
    )(pos, stats, st, e, dp, *blocks)
    rope_part = trade(rope_part, Z + ("y",))
    other = lax.ppermute(other, "y", swap)
    dq_token, *dq = call(
        query_kernel, [TOKEN, ((rows, width), f32)] + [((rows, width), bf16)] * (nx - 1), 2,
        flops=2 * pairs * width, moved=4 * pairs,
    )(ds, keys)
    rope_sum, terms = call(
        weight_kernel, [((k_dev, rope), f32), ((nc * nl * ny * nx, rope, wide), bf16)], 4, unused=(2, 3),
        flops=2 * k_dev * model * rope, moved=4 * k_dev * model, limit=20,
    )(rope_part, cols, other, dq_token)
    terms = trade(terms, ("c", "zl", "y", "x"))
    dq = [dq[0]] + [fetch(dq[k], nx - k, nx) for k in range(1, nx)]
    kept, came = mine, other
    for bit in range(3):
        if bit == 2:
            terms, token = call(
                weight_half_kernel, [((nw * nh, SLOT // 2, 2 * rope), f32), TOKEN], 2, unused=(1,)
            )(terms, token)
            terms = trade(terms, ("w", "zh"))
        n = nz >> (bit + 1)
        kept, sent, token = call(
            functools.partial(halve_kernel, bit), [((n, k_dev, lat), f32), ((n, k_dev, lat), bf16), TOKEN], 4,
            smem=(0,), unused=(3,), flops=8 * n * k_dev * lat, moved=12 * n * k_dev * lat, limit=20,
        )(pos, kept, came, token)
        came = lax.ppermute(sent, Z, [(i, i ^ (1 << bit)) for i in range(nz)])
    (dweight,) = call(weight_sum_kernel, [((block, rope), f32)], 1)(terms)
    (dlatent,) = call(latent_sum_kernel, [((k_dev, width), f32)], 3)(kept, came, rope_sum)

    total = dq[0]
    for part in dq[1:]:
        total = total + part.astype(f32)
    return total.astype(bf16).reshape(query.shape), dlatent[None], dweight


def solution(mesh):
    fine = Mesh(mesh.devices.reshape(4, 2, 4, 2, 2, 4), ("w", "c", "zh", "zl", "y", "x"))
    dp, sp = ("w", "c"), ("zh", "zl", "y", "x")
    tokens = P(dp, sp, None, None)
    keys = P(dp, sp, None)
    return jax.shard_map(
        body,
        mesh=fine,
        in_specs=(tokens, keys, tokens, keys),
        out_specs=(tokens, keys, P(dp + sp, None)),
        check_vma=False,
    )
```

```python
import functools

import jax
import jax.numpy as jnp
from jax import lax
from jax.experimental import pallas as pl
from jax.experimental.pallas import tpu as pltpu
from jax.sharding import Mesh, PartitionSpec as P

softmax_scale = 0.07216878364870323
f32, bf16 = jnp.float32, jnp.bfloat16
TILE = 256
TOKEN = ((8, 128), jnp.float32)
SLOT = 16


def nt(a, b):
    return lax.dot_general(a, b, (((1,), (1,)), ((), ())), preferred_element_type=f32)


def nn(a, b):
    return lax.dot_general(a, b, (((1,), (0,)), ((), ())), preferred_element_type=f32)


def tn(a, b):
    return lax.dot_general(a, b, (((0,), (0,)), ((), ())), preferred_element_type=f32)


def call(kernel, outs, n_in, smem=(), unused=(), scratch=(), flops=0, moved=0, in_hbm=False, limit=20):
    vmem = pl.BlockSpec(memory_space=pltpu.VMEM)
    specs = [
        pl.BlockSpec(memory_space=pltpu.SMEM)
        if i in smem
        else (pl.BlockSpec(memory_space=pl.ANY) if i in unused else vmem)
        for i in range(n_in)
    ]
    return pl.pallas_call(
        kernel,
        out_shape=[pltpu.HBM(s, d) if in_hbm else jax.ShapeDtypeStruct(s, d) for s, d in outs],
        in_specs=specs,
        out_specs=[pl.BlockSpec(memory_space=pltpu.HBM) if in_hbm else vmem] * len(outs),
        scratch_shapes=scratch,
        compiler_params=pltpu.CompilerParams(vmem_limit_bytes=limit * 2**20),
        cost_estimate=pl.CostEstimate(flops=flops, bytes_accessed=moved, transcendentals=0),
    )


def pack_kernel(dout, query, out):
    lat = dout.shape[1]
    width = query.shape[1]
    out[:, :lat] = dout[...]
    out[:, lat : lat + width] = query[...]
    out[:, lat + width :] = jnp.zeros((out.shape[0], out.shape[1] - lat - width), out.dtype)


def latent_copies_kernel(latent, out):
    half = latent.shape[0] // 2
    packed = jnp.concatenate([latent[:half], latent[half:]], axis=1)
    for i in range(out.shape[0]):
        out[i] = packed


def columns_kernel(block, n_z, n_grp, n_core, hid, out, token):
    token[...] = jnp.zeros(token.shape, token.dtype)
    k_dev, model = hid.shape
    n_data = model // (n_z * n_grp * block)
    span = n_z * n_grp * block
    wide = n_z * SLOT
    c = lax.broadcasted_iota(jnp.int32, (span, n_grp * wide), 0)
    o = lax.broadcasted_iota(jnp.int32, (span, n_grp * wide), 1)
    g, zz, k = o // wide, (o % wide) // SLOT, o % SLOT
    pick = jnp.where((c == (zz * n_grp + g) * block + k) & (k < block), 1.0, 0.0).astype(bf16)
    stacked = jnp.concatenate([hid[:, d * span : (d + 1) * span] for d in range(n_data)])
    moved = nn(stacked, pick).astype(bf16)
    for d in range(n_data):
        first = d // n_core * wide
        for g in range(n_grp):
            out[d % n_core * n_grp + g, :, first : first + wide] = moved[
                d * k_dev : (d + 1) * k_dev, g * wide : (g + 1) * wide
            ]


def key_tile(keys, i, per):
    k = keys[i * per : (i + 1) * per]
    return k.reshape(k.shape[0] * k.shape[1], k.shape[2])


def scores_kernel(lat, heads, pos, packed, after, *refs):
    blocks, (e_ref, dp_ref, st_ref, keys) = refs[:-4], refs[-4:]
    wide = keys.shape[2]
    for i in range(keys.shape[0]):
        keys[i] = jnp.concatenate([packed[i, :, :wide], packed[i, :, wide:]])
    z, y, x = pos[0], pos[1], pos[2]
    grp, k_dev, width = keys.shape
    n_x = len(blocks)
    rows = refs[0].shape[0]
    n_keys = grp * k_dev
    tiles = n_keys // TILE
    per = TILE // k_dev
    tok = rows // heads
    first_query = grp * n_x * (k_dev - tok)
    for b, t in enumerate(blocks):
        q, o = t[:, lat : lat + width], t[:, :lat]
        cols = slice(b * rows, (b + 1) * rows)
        lane = lax.broadcasted_iota(jnp.int32, (k_dev, rows), 1)
        q_pos = ((z * 2 + y) * n_x + lax.rem(x + n_x - b, n_x)) * tok + lane // heads + first_query
        top = None
        for i in range(tiles):
            s = nt(key_tile(keys, i, per), q) * softmax_scale
            if i == tiles - 1:
                k_pos = ((grp - 1) * n_x + x) * k_dev + lax.broadcasted_iota(
                    jnp.int32, (k_dev, rows), 0
                )
                last = jnp.where(k_pos <= q_pos, s[TILE - k_dev :], -jnp.inf)
                s = jnp.concatenate([s[: TILE - k_dev], last])
            e_ref[i * TILE : (i + 1) * TILE, cols] = s
            m = jnp.max(s, axis=0, keepdims=True)
            top = m if top is None else jnp.maximum(top, m)
        total = jnp.zeros_like(top)
        delta = jnp.zeros_like(top)
        for i in range(tiles):
            part = slice(i * TILE, (i + 1) * TILE)
            dp = nt(key_tile(keys, i, per)[:, :lat], o)
            e = jnp.exp(e_ref[part, cols] - top)
            e_ref[part, cols] = e
            dp_ref[part, cols] = dp
            total += jnp.sum(e, axis=0, keepdims=True)
            delta += jnp.sum(e * dp, axis=0, keepdims=True)
        st_ref[4 * b : 4 * b + 4] = jnp.concatenate([top, total, delta, jnp.zeros_like(top)])


def dscores_kernel(lat, pos, stats, st, e_ref, dp_ref, *refs):
    n_x = stats.shape[0]
    blocks, outs, (sems, *held) = refs[:n_x], refs[n_x : n_x + 4], refs[n_x + 4 :]
    ds_ref, rope_ref, mine, other, p_ref = held
    copies = [pltpu.make_async_copy(held[i], outs[i], sems.at[i]) for i in range(4)]
    y, x = pos[1], pos[2]
    rows = refs[0].shape[0]
    tiles = e_ref.shape[0] // TILE
    grp, half_keys, _ = rope_ref.shape
    k_dev = 2 * half_keys
    for b in range(n_x):
        cols = slice(b * rows, (b + 1) * rows)
        theirs = []
        for s in range(n_x):
            at = lax.rem(s + b + n_x - x, n_x)
            v = stats[s, 0:4]
            for j in range(1, n_x):
                v = jnp.where(at == j, stats[s, 4 * j : 4 * j + 4], v)
            theirs.append(v)
        top = functools.reduce(jnp.maximum, [v[0:1] for v in theirs])
        w = [jnp.exp(v[0:1] - top) for v in theirs]
        total = sum(v[1:2] * u for v, u in zip(theirs, w))
        delta = sum(v[2:3] * u for v, u in zip(theirs, w)) / total
        f = jnp.exp(st[4 * b : 4 * b + 1] - top) / total
        for i in range(tiles):
            part = slice(i * TILE, (i + 1) * TILE)
            p = e_ref[part, cols] * f
            p_ref[part, cols] = p.astype(bf16)
            ds_ref[part, cols] = (p * (dp_ref[part, cols] - delta)).astype(bf16)
    copies[0].start()
    for i in range(tiles):
        part = slice(i * TILE, (i + 1) * TILE)
        r = None
        for b, t in enumerate(blocks):
            q = t[:, 2 * lat : 2 * lat + rope_ref.shape[2] // 2]
            v = nn(ds_ref[part, b * rows : (b + 1) * rows], q)
            r = v if r is None else r + v
        r = (r * softmax_scale).astype(bf16)
        for j in range(TILE // k_dev):
            k = r[j * k_dev : (j + 1) * k_dev]
            rope_ref[i * (TILE // k_dev) + j] = jnp.concatenate([k[:half_keys], k[half_keys:]], axis=1)
    copies[1].start()
    per = TILE // k_dev
    for i in range(tiles):
        part = slice(i * TILE, (i + 1) * TILE)
        v = None
        for b, t in enumerate(blocks):
            a = nn(ds_ref[part, b * rows : (b + 1) * rows], t[:, lat : 2 * lat])
            v = a if v is None else v + a
        v = v * softmax_scale
        for b, t in enumerate(blocks):
            v += nn(p_ref[part, b * rows : (b + 1) * rows], t[:, :lat])
        v = v.astype(bf16).reshape(per // 2, 2, k_dev, lat)
        first = i * per // 2
        for out, side in ((mine, y), (other, 1 - y)):
            out[first : first + per // 2] = jnp.where(side == 0, v[:, 0], v[:, 1])
    copies[2].start()
    copies[3].start()
    for copy in copies:
        copy.wait()


def query_kernel(ds_ref, keys, token, *outs):
    token[...] = jnp.zeros(token.shape, token.dtype)
    rows = outs[0].shape[0]
    per = TILE // keys.shape[1]
    for b, out in enumerate(outs):
        v = None
        for i in range(ds_ref.shape[0] // TILE):
            a = tn(
                ds_ref[i * TILE : (i + 1) * TILE, b * rows : (b + 1) * rows],
                key_tile(keys, i, per),
            )
            v = a if v is None else v + a
        out[...] = (v * softmax_scale).astype(out.dtype)


def weight_kernel(parts, cols, after, after2, rope_ref, out):
    v = jnp.sum(parts[...].astype(f32), axis=0)
    e = v.shape[1] // 2
    rope = jnp.concatenate([v[:, :e], v[:, e:]])
    rope_ref[...] = rope
    low = rope.astype(bf16)
    for i in range(cols.shape[0]):
        out[i] = tn(low, cols[i]).astype(bf16)


def weight_half_kernel(parts, after, out, token):
    token[...] = jnp.zeros(token.shape, token.dtype)
    v = jnp.sum(parts[...].astype(f32), axis=0)
    v = jnp.swapaxes(v, 0, 1)
    v = v.reshape(v.shape[0] // SLOT, SLOT, v.shape[1])
    out[...] = jnp.concatenate([v[:, : SLOT // 2], v[:, SLOT // 2 :]], axis=2)


def weight_sum_kernel(parts, out):
    v = jnp.sum(parts[...], axis=0)
    e = v.shape[1] // 2
    out[...] = jnp.concatenate([v[:, :e], v[:, e:]])[: out.shape[0]]


def halve_kernel(bit, pos, a, b, after, *refs):
    keep, send, token = refs
    token[...] = jnp.zeros(token.shape, token.dtype)
    mine = (pos[0] >> bit) & 1
    for i in range(keep.shape[0]):
        at, away = 2 * i + mine, 2 * i + 1 - mine
        keep[i] = a[at].astype(f32) + b[at].astype(f32)
        send[i] = (a[away].astype(f32) + b[away].astype(f32)).astype(send.dtype)


def latent_sum_kernel(a, b, rope, out):
    lat = a.shape[2]
    out[:, :lat] = a[0] + b[0].astype(f32)
    out[:, lat:] = rope[...]


def fetch(value, offset, n):
    return lax.ppermute(value, "x", [(s, (s - offset) % n) for s in range(n)])


def trade(value, axes):
    return lax.all_to_all(value, axes, 0, 0, tiled=True)


def body(query, latent, dout, hidden):
    nw, nc, nz, ny, nx = (lax.axis_size(a) for a in ("w", "c", "z", "y", "x"))
    tok, heads, width = query.shape[1:]
    lat = dout.shape[3]
    rope = width - lat
    k_dev, model = hidden.shape[1:]
    rows = tok * heads
    n_rows, n_keys = nx * rows, nz * ny * k_dev
    pairs = n_rows * n_keys
    block = model // (nw * nc * nz * ny * nx)
    swap = [(0, 1), (1, 0)]
    pos = jnp.stack([lax.axis_index(a) for a in ("z", "y", "x")]).astype(jnp.int32)

    (packed,) = call(
        latent_copies_kernel, [((nz * ny, k_dev // 2, 2 * width), bf16)], 1, moved=2 * nz * ny * k_dev * width
    )(latent[0])
    packed = trade(packed, ("z", "y"))
    (own,) = call(pack_kernel, [((rows, -(-(lat + width) // 128) * 128), bf16)], 2, moved=4 * rows * width)(
        dout.reshape(rows, lat), query.reshape(rows, width)
    )
    blocks = [own] + [fetch(own, nx - k, nx) for k in range(1, nx)]

    wide = nw * nz * SLOT
    cols, token = call(
        functools.partial(columns_kernel, block, nz, ny * nx, nc), [((nc * ny * nx, k_dev, wide), bf16), TOKEN], 1,
        flops=2 * k_dev * model * 1024, moved=4 * k_dev * model, limit=20,
    )(hidden[0])
    e, dp, st, keys = call(
        functools.partial(scores_kernel, lat, heads),
        [((n_keys, n_rows), f32)] * 2 + [((4 * nx, rows), f32), ((nz * ny, k_dev, width), bf16)],
        7, smem=(0,),
        unused=(2,),
        flops=2 * pairs * (width + lat), moved=8 * pairs, limit=20,
    )(pos, packed, token, *blocks)
    stats = trade(jnp.broadcast_to(st[None], (nx,) + st.shape), "x")
    ds, rope_part, mine, other = call(
        functools.partial(dscores_kernel, lat),
        [((n_keys, n_rows), bf16), ((nz * ny, k_dev // 2, 2 * rope), bf16)] + [((nz, k_dev, lat), bf16)] * 2,
        9, smem=(0,), in_hbm=True,
        scratch=[
            pltpu.SemaphoreType.DMA((4,)),
            pltpu.VMEM((n_keys, n_rows), bf16),
            pltpu.VMEM((nz * ny, k_dev // 2, 2 * rope), bf16),
            pltpu.VMEM((nz, k_dev, lat), bf16),
            pltpu.VMEM((nz, k_dev, lat), bf16),
            pltpu.VMEM((n_keys, n_rows), bf16),
        ],
        flops=2 * pairs * (rope + 2 * lat), moved=12 * pairs,
    )(pos, stats, st, e, dp, *blocks)
    rope_part = trade(rope_part, ("z", "y"))
    other = lax.ppermute(other, "y", swap)
    dq_token, *dq = call(
        query_kernel, [TOKEN, ((rows, width), f32)] + [((rows, width), bf16)] * (nx - 1), 2,
        flops=2 * pairs * width, moved=4 * pairs,
    )(ds, keys)
    rope_sum, terms = call(
        weight_kernel, [((k_dev, rope), f32), ((nc * ny * nx, rope, wide), bf16)], 4, unused=(2, 3),
        flops=2 * k_dev * nc * ny * nx * wide * rope, moved=4 * k_dev * model, limit=20,
    )(rope_part, cols, other, dq_token)
    terms = trade(terms, ("c", "y", "x"))
    dq = [dq[0]] + [fetch(dq[k], k, nx) for k in range(1, nx)]
    kept, came = mine, other
    for bit in range(3):
        if bit == 2:
            terms, token = call(
                weight_half_kernel, [((nw * nz, SLOT // 2, 2 * rope), f32), TOKEN], 2, unused=(1,)
            )(terms, token)
            terms = trade(terms, ("w", "z"))
        n = nz >> (bit + 1)
        kept, sent, token = call(
            functools.partial(halve_kernel, bit), [((n, k_dev, lat), f32), ((n, k_dev, lat), bf16), TOKEN], 4,
            smem=(0,), unused=(3,), flops=8 * n * k_dev * lat, moved=12 * n * k_dev * lat, limit=20,
        )(pos, kept, came, token)
        came = lax.ppermute(sent, "z", [(i, i ^ (1 << bit)) for i in range(nz)])
    (dweight,) = call(weight_sum_kernel, [((block, rope), f32)], 1)(terms)
    (dlatent,) = call(latent_sum_kernel, [((k_dev, width), f32)], 3)(kept, came, rope_sum)

    total = dq[0]
    for part in dq[1:]:
        total = total + part.astype(f32)
    return total.astype(bf16).reshape(query.shape), dlatent[None], dweight


def solution(mesh):
    fine = Mesh(mesh.devices.reshape(4, 2, 8, 2, 4), ("w", "c", "z", "y", "x"))
    dp, sp = ("w", "c"), ("z", "y", "x")
    tokens = P(dp, sp, None, None)
    keys = P(dp, sp, None)
    return jax.shard_map(
        body,
        mesh=fine,
        in_specs=(tokens, keys, tokens, keys),
        out_specs=(tokens, keys, P(dp + sp, None)),
        check_vma=False,
    )
```

```python
import functools

import jax
import jax.numpy as jnp
from jax import lax
from jax.experimental import pallas as pl
from jax.experimental.pallas import tpu as pltpu
from jax.sharding import Mesh, PartitionSpec as P

softmax_scale = 0.07216878364870323
f32, bf16 = jnp.float32, jnp.bfloat16
TILE = 256
TOKEN = ((8, 128), jnp.float32)
SLOT = 16


def nt(a, b):
    return lax.dot_general(a, b, (((1,), (1,)), ((), ())), preferred_element_type=f32)


def nn(a, b):
    return lax.dot_general(a, b, (((1,), (0,)), ((), ())), preferred_element_type=f32)


def tn(a, b):
    return lax.dot_general(a, b, (((0,), (0,)), ((), ())), preferred_element_type=f32)


def call(kernel, outs, n_in, smem=(), unused=(), scratch=(), flops=0, moved=0, in_hbm=False, limit=20):
    vmem = pl.BlockSpec(memory_space=pltpu.VMEM)
    specs = [
        pl.BlockSpec(memory_space=pltpu.SMEM)
        if i in smem
        else (pl.BlockSpec(memory_space=pl.ANY) if i in unused else vmem)
        for i in range(n_in)
    ]
    return pl.pallas_call(
        kernel,
        out_shape=[pltpu.HBM(s, d) if in_hbm else jax.ShapeDtypeStruct(s, d) for s, d in outs],
        in_specs=specs,
        out_specs=[pl.BlockSpec(memory_space=pltpu.HBM) if in_hbm else vmem] * len(outs),
        scratch_shapes=scratch,
        compiler_params=pltpu.CompilerParams(vmem_limit_bytes=limit * 2**20),
        cost_estimate=pl.CostEstimate(flops=flops, bytes_accessed=moved, transcendentals=0),
    )


def pack_kernel(dout, query, out):
    lat = dout.shape[1]
    width = query.shape[1]
    out[:, :lat] = dout[...]
    out[:, lat : lat + width] = query[...]
    out[:, lat + width :] = jnp.zeros((out.shape[0], out.shape[1] - lat - width), out.dtype)


def columns_kernel(block, n_z, n_grp, n_core, hid, out, token):
    token[...] = jnp.zeros(token.shape, token.dtype)
    k_dev, model = hid.shape
    n_data = model // (n_z * n_grp * block)
    span = n_z * n_grp * block
    wide = n_z * SLOT
    c = lax.broadcasted_iota(jnp.int32, (span, n_grp * wide), 0)
    o = lax.broadcasted_iota(jnp.int32, (span, n_grp * wide), 1)
    g, zz, k = o // wide, (o % wide) // SLOT, o % SLOT
    pick = jnp.where((c == (zz * n_grp + g) * block + k) & (k < block), 1.0, 0.0).astype(bf16)
    stacked = jnp.concatenate([hid[:, d * span : (d + 1) * span] for d in range(n_data)])
    moved = nn(stacked, pick).astype(bf16)
    for d in range(n_data):
        first = d // n_core * wide
        for g in range(n_grp):
            out[d % n_core * n_grp + g, :, first : first + wide] = moved[
                d * k_dev : (d + 1) * k_dev, g * wide : (g + 1) * wide
            ]


def key_tile(keys, i, per):
    k = keys[i * per : (i + 1) * per]
    return k.reshape(k.shape[0] * k.shape[1], k.shape[2])


def scores_kernel(lat, heads, pos, keys, after, *refs):
    blocks, (e_ref, dp_ref, st_ref) = refs[:-3], refs[-3:]
    z, y, x = pos[0], pos[1], pos[2]
    grp, k_dev, width = keys.shape
    n_x = len(blocks)
    rows = refs[0].shape[0]
    n_keys = grp * k_dev
    tiles = n_keys // TILE
    per = TILE // k_dev
    tok = rows // heads
    first_query = grp * n_x * (k_dev - tok)
    for b, t in enumerate(blocks):
        q, o = t[:, lat : lat + width], t[:, :lat]
        cols = slice(b * rows, (b + 1) * rows)
        lane = lax.broadcasted_iota(jnp.int32, (k_dev, rows), 1)
        q_pos = ((z * 2 + y) * n_x + lax.rem(x + b, n_x)) * tok + lane // heads + first_query
        top = None
        for i in range(tiles):
            s = nt(key_tile(keys, i, per), q) * softmax_scale
            if i == tiles - 1:
                k_pos = ((grp - 1) * n_x + x) * k_dev + lax.broadcasted_iota(
                    jnp.int32, (k_dev, rows), 0
                )
                last = jnp.where(k_pos <= q_pos, s[TILE - k_dev :], -jnp.inf)
                s = jnp.concatenate([s[: TILE - k_dev], last])
            e_ref[i * TILE : (i + 1) * TILE, cols] = s
            m = jnp.max(s, axis=0, keepdims=True)
            top = m if top is None else jnp.maximum(top, m)
        total = jnp.zeros_like(top)
        delta = jnp.zeros_like(top)
        for i in range(tiles):
            part = slice(i * TILE, (i + 1) * TILE)
            dp = nt(key_tile(keys, i, per)[:, :lat], o)
            e = jnp.exp(e_ref[part, cols] - top)
            e_ref[part, cols] = e
            dp_ref[part, cols] = dp
            total += jnp.sum(e, axis=0, keepdims=True)
            delta += jnp.sum(e * dp, axis=0, keepdims=True)
        st_ref[4 * b : 4 * b + 4] = jnp.concatenate([top, total, delta, jnp.zeros_like(top)])


def dscores_kernel(lat, pos, stats, st, e_ref, dp_ref, *refs):
    n_x = stats.shape[0]
    blocks, outs, (sems, *held) = refs[:n_x], refs[n_x : n_x + 4], refs[n_x + 4 :]
    ds_ref, rope_ref, _, _, p_ref = held
    y, x = pos[1], pos[2]
    rows = refs[0].shape[0]
    tiles = e_ref.shape[0] // TILE
    grp, half_keys, _ = rope_ref.shape
    k_dev = 2 * half_keys
    factors = []
    for b in range(n_x):
        theirs = []
        for s in range(n_x):
            at = lax.rem(x + b + n_x - s, n_x)
            v = stats[s, 0:4]
            for j in range(1, n_x):
                v = jnp.where(at == j, stats[s, 4 * j : 4 * j + 4], v)
            theirs.append(v)
        top = functools.reduce(jnp.maximum, [v[0:1] for v in theirs])
        w = [jnp.exp(v[0:1] - top) for v in theirs]
        total = sum(v[1:2] * u for v, u in zip(theirs, w))
        delta = sum(v[2:3] * u for v, u in zip(theirs, w)) / total
        f = jnp.exp(st[4 * b : 4 * b + 1] - top) / total
        factors.append((f, delta))
    per = TILE // k_dev
    rope = rope_ref.shape[2] // 2
    copies = []

    def send(which, rows_of):
        copies.append(
            pltpu.make_async_copy(held[which].at[rows_of], outs[which].at[rows_of], sems.at[len(copies)])
        )
        copies[-1].start()

    def weigh(i):
        part = slice(i * TILE, (i + 1) * TILE)
        for b, (f, delta) in enumerate(factors):
            cols = slice(b * rows, (b + 1) * rows)
            p = e_ref[part, cols] * f
            p_ref[part, cols] = p.astype(bf16)
            ds_ref[part, cols] = (p * (dp_ref[part, cols] - delta)).astype(bf16)
        send(0, pl.ds(i * TILE, TILE))

    def multiply(i):
        part = slice(i * TILE, (i + 1) * TILE)
        v = None
        for b, t in enumerate(blocks):
            a = nn(ds_ref[part, b * rows : (b + 1) * rows], t[:, lat : 2 * lat + rope])
            v = a if v is None else v + a
        v = v * softmax_scale
        r, v = v[:, lat:].astype(bf16), v[:, :lat]
        for j in range(per):
            k = r[j * k_dev : (j + 1) * k_dev]
            rope_ref[i * per + j] = jnp.concatenate([k[:half_keys], k[half_keys:]], axis=1)
        for b, t in enumerate(blocks):
            v += nn(p_ref[part, b * rows : (b + 1) * rows], t[:, :lat])
        v = v.astype(bf16).reshape(per // 2, 2, k_dev, lat)
        first = i * per // 2
        for which, side in ((2, y), (3, 1 - y)):
            held[which][first : first + per // 2] = jnp.where(side == 0, v[:, 0], v[:, 1])
            send(which, pl.ds(first, per // 2))

    weigh(0)
    for i in range(tiles):
        if i + 1 < tiles:
            weigh(i + 1)
        multiply(i)
    send(1, pl.ds(0, grp))
    for copy in copies:
        copy.wait()


def query_kernel(ds_ref, keys, token, *outs):
    token[...] = jnp.zeros(token.shape, token.dtype)
    rows = outs[0].shape[0]
    per = TILE // keys.shape[1]
    for b, out in enumerate(outs):
        v = None
        for i in range(ds_ref.shape[0] // TILE):
            a = tn(
                ds_ref[i * TILE : (i + 1) * TILE, b * rows : (b + 1) * rows],
                key_tile(keys, i, per),
            )
            v = a if v is None else v + a
        out[...] = (v * softmax_scale).astype(out.dtype)


def weight_kernel(parts, cols, after, after2, rope_ref, out):
    v = jnp.sum(parts[...].astype(f32), axis=0)
    e = v.shape[1] // 2
    rope = jnp.concatenate([v[:, :e], v[:, e:]])
    rope_ref[...] = rope
    low = rope.astype(bf16)
    for i in range(cols.shape[0]):
        out[i] = tn(low, cols[i]).astype(bf16)


def weight_half_kernel(parts, after, out, token):
    token[...] = jnp.zeros(token.shape, token.dtype)
    v = jnp.sum(parts[...].astype(f32), axis=0)
    v = jnp.swapaxes(v, 0, 1)
    v = v.reshape(v.shape[0] // SLOT, SLOT, v.shape[1])
    out[...] = jnp.concatenate([v[:, : SLOT // 2], v[:, SLOT // 2 :]], axis=2)


def weight_sum_kernel(parts, out):
    v = jnp.sum(parts[...], axis=0)
    e = v.shape[1] // 2
    out[...] = jnp.concatenate([v[:, :e], v[:, e:]])[: out.shape[0]]


def halve_kernel(bit, pos, a, b, after, *refs):
    keep, send, token = refs
    token[...] = jnp.zeros(token.shape, token.dtype)
    mine = (pos[0] >> bit) & 1
    for i in range(keep.shape[0]):
        at, away = 2 * i + mine, 2 * i + 1 - mine
        keep[i] = a[at].astype(f32) + b[at].astype(f32)
        send[i] = (a[away].astype(f32) + b[away].astype(f32)).astype(send.dtype)


def latent_sum_kernel(a, b, rope, after, out):
    lat = a.shape[2]
    out[:, :lat] = a[0] + b[0].astype(f32)
    out[:, lat:] = rope[...]


def fetch(value, offset, n):
    return lax.ppermute(value, "x", [(s, (s - offset) % n) for s in range(n)])


def trade(value, axes):
    return lax.all_to_all(value, axes, 0, 0, tiled=True)


def body(query, latent, dout, hidden):
    nw, nc, nz, ny, nx = (lax.axis_size(a) for a in ("w", "c", "z", "y", "x"))
    tok, heads, width = query.shape[1:]
    lat = dout.shape[3]
    rope = width - lat
    k_dev, model = hidden.shape[1:]
    rows = tok * heads
    n_rows, n_keys = nx * rows, nz * ny * k_dev
    pairs = n_rows * n_keys
    block = model // (nw * nc * nz * ny * nx)
    swap = [(0, 1), (1, 0)]
    pos = jnp.stack([lax.axis_index(a) for a in ("z", "y", "x")]).astype(jnp.int32)

    keys = trade(jnp.broadcast_to(latent, (nz * ny, k_dev, width)), ("z", "y"))
    (own,) = call(pack_kernel, [((rows, -(-(lat + width) // 128) * 128), bf16)], 2, moved=4 * rows * width)(
        dout.reshape(rows, lat), query.reshape(rows, width)
    )
    blocks = [own] + [fetch(own, k, nx) for k in range(1, nx)]

    wide = nw * nz * SLOT
    cols, token = call(
        functools.partial(columns_kernel, block, nz, ny * nx, nc), [((nc * ny * nx, k_dev, wide), bf16), TOKEN], 1,
        flops=2 * k_dev * model * 1024, moved=4 * k_dev * model, limit=20,
    )(hidden[0])
    e, dp, st = call(
        functools.partial(scores_kernel, lat, heads),
        [((n_keys, n_rows), f32)] * 2 + [((4 * nx, rows), f32)], 7, smem=(0,),
        unused=(2,),
        flops=2 * pairs * (width + lat), moved=8 * pairs, limit=20,
    )(pos, keys, token, *blocks)
    stats = trade(jnp.broadcast_to(st[None], (nx,) + st.shape), "x")
    ds, rope_part, mine, other = call(
        functools.partial(dscores_kernel, lat),
        [((n_keys, n_rows), bf16), ((nz * ny, k_dev // 2, 2 * rope), bf16)] + [((nz, k_dev, lat), bf16)] * 2,
        9, smem=(0,), in_hbm=True,
        scratch=[
            pltpu.SemaphoreType.DMA((3 * n_keys // TILE + 1,)),
            pltpu.VMEM((n_keys, n_rows), bf16),
            pltpu.VMEM((nz * ny, k_dev // 2, 2 * rope), bf16),
            pltpu.VMEM((nz, k_dev, lat), bf16),
            pltpu.VMEM((nz, k_dev, lat), bf16),
            pltpu.VMEM((n_keys, n_rows), bf16),
        ],
        flops=2 * pairs * (rope + 2 * lat), moved=12 * pairs,
    )(pos, stats, st, e, dp, *blocks)
    rope_part = trade(rope_part, ("z", "y"))
    other = lax.ppermute(other, "y", swap)
    dq_token, *dq = call(
        query_kernel, [TOKEN, ((rows, width), f32)] + [((rows, width), bf16)] * (nx - 1), 2,
        flops=2 * pairs * width, moved=4 * pairs,
    )(ds, keys)
    rope_sum, terms = call(
        weight_kernel, [((k_dev, rope), f32), ((nc * ny * nx, rope, wide), bf16)], 4, unused=(2, 3),
        flops=2 * k_dev * nc * ny * nx * wide * rope, moved=4 * k_dev * model, limit=20,
    )(rope_part, cols, other, dq_token)
    terms = trade(terms, ("c", "y", "x"))
    dq = [dq[0]] + [fetch(dq[k], nx - k, nx) for k in range(1, nx)]
    kept, came = mine, other
    for bit in range(3):
        if bit == 2:
            terms, token = call(
                weight_half_kernel, [((nw * nz, SLOT // 2, 2 * rope), f32), TOKEN], 2, unused=(1,)
            )(terms, token)
            terms = trade(terms, ("w", "z"))
        n = nz >> (bit + 1)
        kept, sent, token = call(
            functools.partial(halve_kernel, bit), [((n, k_dev, lat), f32), ((n, k_dev, lat), bf16), TOKEN], 4,
            smem=(0,), unused=(3,), flops=8 * n * k_dev * lat, moved=12 * n * k_dev * lat, limit=20,
        )(pos, kept, came, token)
        came = lax.ppermute(sent, "z", [(i, i ^ (1 << bit)) for i in range(nz)])
    (dweight,) = call(weight_sum_kernel, [((block, rope), f32)], 1)(terms)
    (dlatent,) = call(latent_sum_kernel, [((k_dev, width), f32)], 4, unused=(3,))(kept, came, rope_sum, dweight)

    total = dq[0]
    for part in dq[1:]:
        total = total + part.astype(f32)
    return total.astype(bf16).reshape(query.shape), dlatent[None], dweight


def solution(mesh):
    fine = Mesh(mesh.devices.reshape(4, 2, 8, 2, 4), ("w", "c", "z", "y", "x"))
    dp, sp = ("w", "c"), ("z", "y", "x")
    tokens = P(dp, sp, None, None)
    keys = P(dp, sp, None)
    return jax.shard_map(
        body,
        mesh=fine,
        in_specs=(tokens, keys, tokens, keys),
        out_specs=(tokens, keys, P(dp + sp, None)),
        check_vma=False,
    )
```

```python
import functools

import jax
import jax.numpy as jnp
from jax import lax
from jax.experimental import pallas as pl
from jax.experimental.pallas import tpu as pltpu
from jax.sharding import Mesh, PartitionSpec as P

softmax_scale = 0.07216878364870323
f32, bf16 = jnp.float32, jnp.bfloat16
TILE = 256
TOKEN = ((8, 128), jnp.float32)
SLOT = 16


def nt(a, b):
    return lax.dot_general(a, b, (((1,), (1,)), ((), ())), preferred_element_type=f32)


def nn(a, b):
    return lax.dot_general(a, b, (((1,), (0,)), ((), ())), preferred_element_type=f32)


def tn(a, b):
    return lax.dot_general(a, b, (((0,), (0,)), ((), ())), preferred_element_type=f32)


def call(kernel, outs, n_in, smem=(), unused=(), scratch=(), flops=0, moved=0, in_hbm=False, limit=20):
    vmem = pl.BlockSpec(memory_space=pltpu.VMEM)
    specs = [
        pl.BlockSpec(memory_space=pltpu.SMEM)
        if i in smem
        else (pl.BlockSpec(memory_space=pl.ANY) if i in unused else vmem)
        for i in range(n_in)
    ]
    return pl.pallas_call(
        kernel,
        out_shape=[pltpu.HBM(s, d) if in_hbm else jax.ShapeDtypeStruct(s, d) for s, d in outs],
        in_specs=specs,
        out_specs=[pl.BlockSpec(memory_space=pltpu.HBM) if in_hbm else vmem] * len(outs),
        scratch_shapes=scratch,
        compiler_params=pltpu.CompilerParams(vmem_limit_bytes=limit * 2**20),
        cost_estimate=pl.CostEstimate(flops=flops, bytes_accessed=moved, transcendentals=0),
    )


def pack_kernel(dout, query, out):
    lat = dout.shape[1]
    width = query.shape[1]
    out[:, :lat] = dout[...]
    out[:, lat : lat + width] = query[...]
    out[:, lat + width :] = jnp.zeros((out.shape[0], out.shape[1] - lat - width), out.dtype)


def columns_kernel(block, n_z, n_grp, n_core, hid, out, token):
    token[...] = jnp.zeros(token.shape, token.dtype)
    k_dev, model = hid.shape
    n_data = model // (n_z * n_grp * block)
    span = n_z * n_grp * block
    wide = n_z * SLOT
    c = lax.broadcasted_iota(jnp.int32, (span, n_grp * wide), 0)
    o = lax.broadcasted_iota(jnp.int32, (span, n_grp * wide), 1)
    g, zz, k = o // wide, (o % wide) // SLOT, o % SLOT
    pick = jnp.where((c == (zz * n_grp + g) * block + k) & (k < block), 1.0, 0.0).astype(bf16)
    stacked = jnp.concatenate([hid[:, d * span : (d + 1) * span] for d in range(n_data)])
    moved = nn(stacked, pick).astype(bf16)
    for d in range(n_data):
        first = d // n_core * wide
        for g in range(n_grp):
            out[d % n_core * n_grp + g, :, first : first + wide] = moved[
                d * k_dev : (d + 1) * k_dev, g * wide : (g + 1) * wide
            ]


def key_tile(keys, i, per):
    k = keys[i * per : (i + 1) * per]
    return k.reshape(k.shape[0] * k.shape[1], k.shape[2])


def scores_kernel(lat, heads, pos, keys, after, *refs):
    blocks, (e_ref, dp_ref, st_ref) = refs[:-3], refs[-3:]
    z, y, x = pos[0], pos[1], pos[2]
    grp, k_dev, width = keys.shape
    n_x = len(blocks)
    rows = refs[0].shape[0]
    n_keys = grp * k_dev
    tiles = n_keys // TILE
    per = TILE // k_dev
    tok = rows // heads
    first_query = grp * n_x * (k_dev - tok)
    for b, t in enumerate(blocks):
        q, o = t[:, lat : lat + width], t[:, :lat]
        cols = slice(b * rows, (b + 1) * rows)
        lane = lax.broadcasted_iota(jnp.int32, (k_dev, rows), 1)
        q_pos = ((z * 2 + y) * n_x + lax.rem(x + b, n_x)) * tok + lane // heads + first_query
        top = None
        for i in range(tiles):
            s = nt(key_tile(keys, i, per), q) * softmax_scale
            if i == tiles - 1:
                k_pos = ((grp - 1) * n_x + x) * k_dev + lax.broadcasted_iota(
                    jnp.int32, (k_dev, rows), 0
                )
                last = jnp.where(k_pos <= q_pos, s[TILE - k_dev :], -jnp.inf)
                s = jnp.concatenate([s[: TILE - k_dev], last])
            e_ref[i * TILE : (i + 1) * TILE, cols] = s
            m = jnp.max(s, axis=0, keepdims=True)
            top = m if top is None else jnp.maximum(top, m)
        total = jnp.zeros_like(top)
        delta = jnp.zeros_like(top)
        for i in range(tiles):
            part = slice(i * TILE, (i + 1) * TILE)
            dp = nt(key_tile(keys, i, per)[:, :lat], o)
            e = jnp.exp(e_ref[part, cols] - top)
            e_ref[part, cols] = e
            dp_ref[part, cols] = dp
            total += jnp.sum(e, axis=0, keepdims=True)
            delta += jnp.sum(e * dp, axis=0, keepdims=True)
        st_ref[4 * b : 4 * b + 4] = jnp.concatenate([top, total, delta, jnp.zeros_like(top)])


def dscores_kernel(lat, pos, stats, st, e_ref, dp_ref, *refs):
    n_x = stats.shape[0]
    blocks, outs, (sems, *held) = refs[:n_x], refs[n_x : n_x + 4], refs[n_x + 4 :]
    ds_ref, rope_ref, _, _, p_ref = held
    y, x = pos[1], pos[2]
    rows = refs[0].shape[0]
    tiles = e_ref.shape[0] // TILE
    grp, half_keys, _ = rope_ref.shape
    k_dev = 2 * half_keys
    factors = []
    for b in range(n_x):
        theirs = []
        for s in range(n_x):
            at = lax.rem(x + b + n_x - s, n_x)
            v = stats[s, 0:4]
            for j in range(1, n_x):
                v = jnp.where(at == j, stats[s, 4 * j : 4 * j + 4], v)
            theirs.append(v)
        top = functools.reduce(jnp.maximum, [v[0:1] for v in theirs])
        w = [jnp.exp(v[0:1] - top) for v in theirs]
        total = sum(v[1:2] * u for v, u in zip(theirs, w))
        delta = sum(v[2:3] * u for v, u in zip(theirs, w)) / total
        f = jnp.exp(st[4 * b : 4 * b + 1] - top) / total
        factors.append((f, delta))
    per = TILE // k_dev
    rope = rope_ref.shape[2] // 2
    copies = []

    def send(which, rows_of):
        copies.append(
            pltpu.make_async_copy(held[which].at[rows_of], outs[which].at[rows_of], sems.at[len(copies)])
        )
        copies[-1].start()

    def weigh(i):
        part = slice(i * TILE, (i + 1) * TILE)
        for b, (f, delta) in enumerate(factors):
            cols = slice(b * rows, (b + 1) * rows)
            p = e_ref[part, cols] * f
            p_ref[part, cols] = p.astype(bf16)
            ds_ref[part, cols] = (p * (dp_ref[part, cols] - delta)).astype(bf16)
        send(0, pl.ds(i * TILE, TILE))

    def multiply(i):
        part = slice(i * TILE, (i + 1) * TILE)
        v = None
        for b, t in enumerate(blocks):
            a = nn(ds_ref[part, b * rows : (b + 1) * rows], t[:, lat : 2 * lat + rope])
            v = a if v is None else v + a
        v = v * softmax_scale
        r, v = v[:, lat:].astype(bf16), v[:, :lat]
        for j in range(per):
            k = r[j * k_dev : (j + 1) * k_dev]
            rope_ref[i * per + j] = jnp.concatenate([k[:half_keys], k[half_keys:]], axis=1)
        for b, t in enumerate(blocks):
            v += nn(p_ref[part, b * rows : (b + 1) * rows], t[:, :lat])
        v = v.astype(bf16).reshape(per // 2, 2, k_dev, lat)
        first = i * per // 2
        for which, side in ((2, y), (3, 1 - y)):
            held[which][first : first + per // 2] = jnp.where(side == 0, v[:, 0], v[:, 1])
            send(which, pl.ds(first, per // 2))

    weigh(0)
    for i in range(tiles):
        if i + 1 < tiles:
            weigh(i + 1)
        multiply(i)
    send(1, pl.ds(0, grp))
    for copy in copies:
        copy.wait()


def query_kernel(ds_ref, keys, token, *outs):
    token[...] = jnp.zeros(token.shape, token.dtype)
    rows = outs[0].shape[0]
    per = TILE // keys.shape[1]
    for b, out in enumerate(outs):
        v = None
        for i in range(ds_ref.shape[0] // TILE):
            a = tn(
                ds_ref[i * TILE : (i + 1) * TILE, b * rows : (b + 1) * rows],
                key_tile(keys, i, per),
            )
            v = a if v is None else v + a
        out[...] = (v * softmax_scale).astype(out.dtype)


def weight_kernel(parts, cols, after, after2, rope_ref, out):
    v = jnp.sum(parts[...].astype(f32), axis=0)
    e = v.shape[1] // 2
    rope = jnp.concatenate([v[:, :e], v[:, e:]])
    rope_ref[...] = rope
    low = rope.astype(bf16)
    for i in range(cols.shape[0]):
        out[i] = tn(low, cols[i]).astype(bf16)


def weight_half_kernel(parts, after, out, token):
    token[...] = jnp.zeros(token.shape, token.dtype)
    v = jnp.sum(parts[...].astype(f32), axis=0)
    v = jnp.swapaxes(v, 0, 1)
    v = v.reshape(v.shape[0] // SLOT, SLOT, v.shape[1])
    out[...] = jnp.concatenate([v[:, : SLOT // 2], v[:, SLOT // 2 :]], axis=2)


def weight_sum_kernel(parts, out):
    v = jnp.sum(parts[...], axis=0)
    e = v.shape[1] // 2
    out[...] = jnp.concatenate([v[:, :e], v[:, e:]])[: out.shape[0]]


def halve_kernel(bit, pos, a, b, after, *refs):
    keep, send, token = refs
    token[...] = jnp.zeros(token.shape, token.dtype)
    mine = (pos[0] >> bit) & 1
    for i in range(keep.shape[0]):
        at, away = 2 * i + mine, 2 * i + 1 - mine
        keep[i] = a[at].astype(f32) + b[at].astype(f32)
        send[i] = (a[away].astype(f32) + b[away].astype(f32)).astype(send.dtype)


def latent_sum_kernel(a, b, rope, out):
    lat = a.shape[2]
    out[:, :lat] = a[0] + b[0].astype(f32)
    out[:, lat:] = rope[...]


def fetch(value, offset, n):
    return lax.ppermute(value, "x", [(s, (s - offset) % n) for s in range(n)])


def trade(value, axes):
    return lax.all_to_all(value, axes, 0, 0, tiled=True)


def body(query, latent, dout, hidden):
    nw, nc, nz, ny, nx = (lax.axis_size(a) for a in ("w", "c", "z", "y", "x"))
    tok, heads, width = query.shape[1:]
    lat = dout.shape[3]
    rope = width - lat
    k_dev, model = hidden.shape[1:]
    rows = tok * heads
    n_rows, n_keys = nx * rows, nz * ny * k_dev
    pairs = n_rows * n_keys
    block = model // (nw * nc * nz * ny * nx)
    swap = [(0, 1), (1, 0)]
    pos = jnp.stack([lax.axis_index(a) for a in ("z", "y", "x")]).astype(jnp.int32)

    keys = trade(jnp.broadcast_to(latent, (nz * ny, k_dev, width)), ("z", "y"))
    (own,) = call(pack_kernel, [((rows, -(-(lat + width) // 128) * 128), bf16)], 2, moved=4 * rows * width)(
        dout.reshape(rows, lat), query.reshape(rows, width)
    )
    blocks = [own] + [fetch(own, k, nx) for k in range(1, nx)]

    wide = nw * nz * SLOT
    cols, token = call(
        functools.partial(columns_kernel, block, nz, ny * nx, nc), [((nc * ny * nx, k_dev, wide), bf16), TOKEN], 1,
        flops=2 * k_dev * model * 1024, moved=4 * k_dev * model, limit=20,
    )(hidden[0])
    e, dp, st = call(
        functools.partial(scores_kernel, lat, heads),
        [((n_keys, n_rows), f32)] * 2 + [((4 * nx, rows), f32)], 7, smem=(0,),
        unused=(2,),
        flops=2 * pairs * (width + lat), moved=8 * pairs, limit=20,
    )(pos, keys, token, *blocks)
    stats = trade(jnp.broadcast_to(st[None], (nx,) + st.shape), "x")
    ds, rope_part, mine, other = call(
        functools.partial(dscores_kernel, lat),
        [((n_keys, n_rows), bf16), ((nz * ny, k_dev // 2, 2 * rope), bf16)] + [((nz, k_dev, lat), bf16)] * 2,
        9, smem=(0,), in_hbm=True,
        scratch=[
            pltpu.SemaphoreType.DMA((3 * n_keys // TILE + 1,)),
            pltpu.VMEM((n_keys, n_rows), bf16),
            pltpu.VMEM((nz * ny, k_dev // 2, 2 * rope), bf16),
            pltpu.VMEM((nz, k_dev, lat), bf16),
            pltpu.VMEM((nz, k_dev, lat), bf16),
            pltpu.VMEM((n_keys, n_rows), bf16),
        ],
        flops=2 * pairs * (rope + 2 * lat), moved=12 * pairs,
    )(pos, stats, st, e, dp, *blocks)
    rope_part = trade(rope_part, ("z", "y"))
    other = lax.ppermute(other, "y", swap)
    dq_token, *dq = call(
        query_kernel, [TOKEN, ((rows, width), f32)] + [((rows, width), bf16)] * (nx - 1), 2,
        flops=2 * pairs * width, moved=4 * pairs,
    )(ds, keys)
    rope_sum, terms = call(
        weight_kernel, [((k_dev, rope), f32), ((nc * ny * nx, rope, wide), bf16)], 4, unused=(2, 3),
        flops=2 * k_dev * nc * ny * nx * wide * rope, moved=4 * k_dev * model, limit=20,
    )(rope_part, cols, other, dq_token)
    terms = trade(terms, ("c", "y", "x"))
    dq = [dq[0]] + [fetch(dq[k], nx - k, nx) for k in range(1, nx)]
    kept, came = mine, other
    for bit in range(3):
        if bit == 2:
            terms, token = call(
                weight_half_kernel, [((nw * nz, SLOT // 2, 2 * rope), f32), TOKEN], 2, unused=(1,)
            )(terms, token)
            terms = trade(terms, ("w", "z"))
        n = nz >> (bit + 1)
        kept, sent, token = call(
            functools.partial(halve_kernel, bit), [((n, k_dev, lat), f32), ((n, k_dev, lat), bf16), TOKEN], 4,
            smem=(0,), unused=(3,), flops=8 * n * k_dev * lat, moved=12 * n * k_dev * lat, limit=20,
        )(pos, kept, came, token)
        came = lax.ppermute(sent, "z", [(i, i ^ (1 << bit)) for i in range(nz)])
    (dweight,) = call(weight_sum_kernel, [((block, rope), f32)], 1)(terms)
    (dlatent,) = call(latent_sum_kernel, [((k_dev, width), f32)], 3)(kept, came, rope_sum)

    total = dq[0]
    for part in dq[1:]:
        total = total + part.astype(f32)
    return total.astype(bf16).reshape(query.shape), dlatent[None], dweight


def solution(mesh):
    fine = Mesh(mesh.devices.reshape(4, 2, 8, 2, 4), ("w", "c", "z", "y", "x"))
    dp, sp = ("w", "c"), ("z", "y", "x")
    tokens = P(dp, sp, None, None)
    keys = P(dp, sp, None)
    return jax.shard_map(
        body,
        mesh=fine,
        in_specs=(tokens, keys, tokens, keys),
        out_specs=(tokens, keys, P(dp + sp, None)),
        check_vma=False,
    )
```
